512 devices in a mesh: ctx: 32 (over y, x, core), exp: 16 (over z).
Axes of the slice: x: 4, y: 4, z: 16, core: 2. Of those that a mesh axis runs over, the one named last changes fastest.
Arguments:
- hidden: bfloat16 [128, 32, 7168], P('exp', None, 'ctx'), may hold values from -60 to 60
- routes: int32 [128, 32, 8], P('exp'), may hold values from 0 to 255, as said below
- gates: float32 [128, 32, 8], P('exp'), may hold values from 0.4 to 2
- moe_gain: float32 [7168], P('ctx'), may hold values from 0.25 to 1.75
- gate_weight: bfloat16 [16, 7168, 2048], P('exp', 'ctx'), may hold values from -0.125 to 0.125
- up_weight: bfloat16 [16, 7168, 2048], P('exp', 'ctx'), may hold values from -0.125 to 0.125
- down_weight: bfloat16 [16, 2048, 7168], P('exp', None, 'ctx'), may hold values from -0.125 to 0.125
- latent_weight: bfloat16 [7168, 512], P('ctx'), may hold values from -2 to 2
- latent_gain: float32 [512], replicated, may hold values from 0.25 to 1.75
- queries: bfloat16 [4096, 64, 512], P('ctx', 'exp'), may hold values from -280 to 280
- subtree_end: int32 [4096], replicated, may hold values from 512 to 4095, as said below
Outputs:
- next_hidden: bfloat16 [128, 32, 7168], P('exp', None, 'ctx')
- attn_out: bfloat16 [4096, 64, 512], P('ctx', 'exp')
The draws below stay inside these ranges and needn't reach their ends.
Inputs may be any that keep to these rules, and one draw needn't show every extreme that they name: `routes`: each row names 8 different experts, at most one of them below 16. In the rows of one index of exp (aligned blocks of 256 rows in the order of the first two dimensions) no expert below 16 is named by more than 12 rows, and in every block some expert below 16 is named by exactly 12 rows. subtree_end[j] is the last position of the subtree of token j in a tree laid out in depth-first order, so subtree_end[j] >= j. The first 512 tokens form a chain from which every later token descends; the rest splits into runs of 512 consecutive tokens, each a subtree of its own.
All inputs are finite; a program needn't handle non-finite values.
Results may differ from the reference program's by a relative error of at most 0.033.
Values may be sent and summed in bfloat16 or wider, within the bound.
No kernel may reach another device: no remote copies, remote signals or barrier semaphores. Data moves between devices by JAX's collectives and lax.ppermute only.
A program may use at most 64 MiB of HBM per device.

```python
import math
import jax
import jax.numpy as jnp
from jax import lax

D = 7168
F = 2048
LATENT = 512
HEADS = 64
EXPERTS_ALL = 256
TOP = 8
PROMPT_BLK = 4
GROUP_BLK = 4
TOK_DEV = 128
TOKENS = 4096
TOK_MOE = 256
EXPERTS = 16
CAP = 12
N_CTX = 32
N_EXP = 16


def draw_hidden(key, part):
    key = jax.random.fold_in(key, 11)
    sub_keys = jax.random.split(key, 3)
    full_shape = (TOK_DEV, TOKENS // TOK_DEV, D)
    position = jnp.arange(D, dtype=jnp.float32) / D
    rough_scale = jnp.exp(jax.random.uniform(sub_keys[1], (D,), jnp.float32) * math.log(3.3))
    row_scale = jnp.exp(jax.random.uniform(sub_keys[2], (TOK_DEV, TOKENS // TOK_DEV, 1), jnp.float32, math.log(0.4), math.log(4.0)))
    base_values = jnp.clip(jax.random.normal(sub_keys[0], full_shape, jnp.float32), -4.0, 4.0)
    column = 0.25 * jnp.power(3.0, position) * rough_scale
    return (base_values * row_scale * column).astype(jnp.bfloat16)


def draw_latent_weight(key, part):
    key = jax.random.fold_in(key, 41)
    sub_keys = jax.random.split(key, 2)
    column = jnp.exp(jax.random.uniform(sub_keys[1], (LATENT,), jnp.float32) * math.log(10.0)) / math.sqrt(10.0)
    base_values = jnp.clip(jax.random.normal(sub_keys[0], (D, LATENT), jnp.float32), -5.0, 5.0)
    return (base_values * column[None, :] * D ** (-0.5)).astype(jnp.bfloat16)


def draw_queries(key, part):
    key = jax.random.fold_in(key, 53)
    sub_keys = jax.random.split(key, 1)
    full_shape = (TOKENS, HEADS, LATENT)
    return (2.0 * jnp.clip(jax.random.normal(sub_keys[0], full_shape, jnp.float32), -6.0, 6.0)).astype(jnp.bfloat16)


def draw_subtree_end(key, part):
    key = jax.random.fold_in(key, 67)
    sub_keys = jax.random.split(key, 2)
    prompt_len = PROMPT_BLK * TOK_DEV
    group_len = GROUP_BLK * TOK_DEV
    group_total = (TOKENS - prompt_len) // group_len
    position = jnp.arange(TOKENS, dtype=jnp.int32)
    group_id = jnp.clip((position - prompt_len) // group_len, 0, group_total - 1)
    group_first = prompt_len + group_id * group_len
    offset = position - group_first
    shared = jax.random.randint(sub_keys[0], (group_total,), 1, group_len // 2 + 1)
    chain_len = shared[group_id]
    split_here = jax.random.randint(sub_keys[1], (TOKENS,), 0, TOK_DEV) == 0
    branch_start = (offset == chain_len) | (offset == 0) | (offset > chain_len) & split_here
    candidate = jnp.where(branch_start, position, TOKENS).astype(jnp.int32)
    later = jnp.concatenate([candidate[1:], jnp.full((1,), TOKENS, jnp.int32)])
    next_start = lax.cummin(later, axis=0, reverse=True)
    group_end = group_first + group_len - 1
    tree_end = jnp.where(offset < chain_len, group_end, next_start - 1)
    tree_end = jnp.where(position < prompt_len, TOKENS - 1, tree_end)
    return tree_end.astype(jnp.int32)


def draw_routes(key, part):
    key = jax.random.fold_in(key, 79)
    sub_keys = jax.random.split(key, 6)
    block_total = TOKENS // TOK_MOE
    counts = jax.random.randint(sub_keys[0], (block_total, EXPERTS), CAP // 3, CAP + 1)
    busiest = jax.random.randint(sub_keys[1], (block_total, 1), 0, EXPERTS)
    always_full = jax.random.randint(sub_keys[2], (), 0, EXPERTS)
    expert_range = jnp.arange(EXPERTS, dtype=jnp.int32)
    filled = (expert_range[None, :] == busiest) | (expert_range[None, :] == always_full)
    counts = jnp.where(filled, CAP, counts).astype(jnp.int32)
    upper = jnp.cumsum(counts, axis=1).astype(jnp.int32)
    lower = upper - counts
    places = jnp.arange(TOK_MOE, dtype=jnp.int32)
    inside = (places[None, :, None] >= lower[:, None, :]) & (places[None, :, None] < upper[:, None, :])
    has_window = jnp.any(inside, axis=2)
    window_id = jnp.sum(jnp.where(inside, expert_range[None, None, :], 0), axis=2).astype(jnp.int32)
    orders = jax.vmap(lambda block_key: jax.random.permutation(block_key, TOK_MOE))(jax.random.split(sub_keys[3], block_total))
    inverse = jnp.argsort(orders, axis=1, stable=True)
    has_window = jnp.take_along_axis(has_window, inverse, axis=1)
    window_id = jnp.take_along_axis(window_id, inverse, axis=1)
    other_count = EXPERTS_ALL - EXPERTS
    ranked = jax.random.randint(sub_keys[4], (block_total, TOK_MOE, other_count), 0, 2 ** 20) * other_count + jnp.arange(other_count, dtype=jnp.int32)
    others = lax.top_k(ranked, TOP)[1].astype(jnp.int32) + EXPERTS
    slot_pick = jax.random.randint(sub_keys[5], (block_total, TOK_MOE, 1), 0, TOP)
    use_window = (jnp.arange(TOP, dtype=jnp.int32)[None, None, :] == slot_pick) & has_window[:, :, None]
    chosen = jnp.where(use_window, window_id[:, :, None], others)
    return chosen.reshape(TOK_DEV, TOKENS // TOK_DEV, TOP).astype(jnp.int32)


def strengthened(drawn, stream_key, source, target, blocks, factor):
    owner, partner = [(jnp.arange(drawn.shape[dim]) // (drawn.shape[dim] // blocks)).reshape([-1 if axis == dim else 1 for axis in range(drawn.ndim)]) for dim in (source, target)]
    chosen = jax.random.permutation(stream_key, blocks)[partner]
    strong = (owner == chosen) | (owner == (partner + blocks // 2) % blocks)
    return jnp.where(strong, factor * drawn, drawn)


def levels(own_key, shape, cuts, smallest, largest):
    def one(axis_at, shards_of):
        draws = jax.random.uniform(jax.random.fold_in(jax.random.fold_in(own_key, 6), axis_at), (shards_of,), jnp.float32, smallest / len(cuts), largest / len(cuts))
        return jnp.repeat(jnp.exp(draws), shape[axis_at] // shards_of).reshape((-1,) + (1,) * (len(shape) - axis_at - 1))

    factor_of = one(*cuts[0])
    for cut in cuts[1:]:
        factor_of = factor_of * one(*cut)
    return factor_of


def centred(own_key, shape, spread, most, pieces=(), kind=jnp.bfloat16):
    level = levels(own_key, shape, pieces, -0.22, 0.18) if pieces else 1.0
    result = jax.random.normal(own_key, shape, jnp.float32) * spread * level
    return jnp.minimum(jnp.maximum(result, -most), most).astype(kind)


def noise_with(own_key, shape, deviation, limit, cuts, heavy, kind=jnp.bfloat16):
    values = deviation * jax.random.normal(own_key, shape, jnp.float32)
    if cuts:
        values = values * levels(own_key, shape, cuts, -0.22, 0.18)
    return jnp.clip(strengthened(values, jax.random.fold_in(own_key, 3), *heavy), -limit, limit).astype(kind)


def setup_inputs(seed: int = 0) -> dict:
    arg_keys = jax.random.split(jax.random.key(seed), 12)
    hidden = draw_hidden(jax.random.fold_in(arg_keys[11], 71), 0)
    routes = draw_routes(jax.random.fold_in(arg_keys[11], 71), 0)
    gates = jnp.clip(0.4 + 1.6 * jax.random.uniform(arg_keys[2], (TOK_DEV, N_CTX, TOP), jnp.float32) ** levels(arg_keys[2], (TOK_DEV, N_CTX, TOP), ((0, 16),), -0.2, 0.2), 0.4, 2.0)
    moe_gain = jnp.clip(1.0 + 0.15 * jax.random.normal(arg_keys[3], (D,), jnp.float32), 0.25, 1.75)
    gate_weight = noise_with(arg_keys[4], (EXPERTS, D, F), D ** -0.5, 0.125, ((0, 16), (1, 32)), (1, 2, 32, 2.75))
    up_weight = noise_with(arg_keys[5], (EXPERTS, D, F), D ** -0.5, 0.125, ((0, 16), (1, 32)), (1, 2, 32, 2.75))
    down_weight = centred(arg_keys[6], (EXPERTS, F, D), F ** -0.5, 0.125, ((0, 16), (2, 32)))
    latent_weight = draw_latent_weight(jax.random.fold_in(arg_keys[11], 71), 0)
    latent_gain = jnp.clip(1.0 + 0.15 * jax.random.normal(arg_keys[8], (LATENT,), jnp.float32), 0.25, 1.75)
    queries = draw_queries(jax.random.fold_in(arg_keys[11], 71), 0)
    subtree_end = draw_subtree_end(jax.random.fold_in(arg_keys[11], 71), 0)
    return {"hidden": hidden, "routes": routes, "gates": gates, "moe_gain": moe_gain, "gate_weight": gate_weight, "up_weight": up_weight, "down_weight": down_weight, "latent_weight": latent_weight, "latent_gain": latent_gain, "queries": queries, "subtree_end": subtree_end}


score_scale = 192 ** (-0.5)
norm_eps = 1e-06

def expert_forward(token_rows, gate_matrix, up_matrix, down_matrix):
    gate_value = jnp.dot(token_rows, gate_matrix, preferred_element_type=jnp.float32)
    up_value = jnp.dot(token_rows, up_matrix, preferred_element_type=jnp.float32)
    activated = (jax.nn.silu(gate_value) * up_value).astype(jnp.bfloat16)
    return jnp.dot(activated, down_matrix, preferred_element_type=jnp.float32).astype(jnp.bfloat16)

def reference(hidden, routes, gates, moe_gain, gate_weight, up_weight, down_weight, latent_weight, latent_gain, queries, subtree_end):
    flat_hidden = hidden.reshape(TOKENS, D).astype(jnp.float32)
    inv_rms = lax.rsqrt(lax.optimization_barrier(jnp.mean(flat_hidden * flat_hidden, axis=1, keepdims=True)) + norm_eps)
    normed = (flat_hidden * inv_rms * moe_gain[None, :]).astype(jnp.bfloat16)
    route_ids = routes.reshape(TOKENS, TOP)
    route_gates = gates.reshape(TOKENS, TOP)
    slot_total = N_EXP * CAP
    token_range = jnp.arange(TOKENS, dtype=jnp.int32)

    def one_expert(moe_sum, expert_id):
        matched = route_ids == expert_id
        chosen = jnp.any(matched, axis=1)
        gate_value = lax.optimization_barrier(jnp.sum(jnp.where(matched, route_gates, 0.0), axis=1))
        position = (jnp.cumsum(chosen.astype(jnp.int32)) - 1).astype(jnp.int32)
        target = jnp.where(chosen, position, slot_total).astype(jnp.int32)
        index_list = jnp.zeros((slot_total,), jnp.int32).at[target].set(token_range, mode='drop')
        expert_out = expert_forward(normed[index_list], gate_weight[expert_id], up_weight[expert_id], down_weight[expert_id])
        returned = expert_out[jnp.clip(position, 0, slot_total - 1)].astype(jnp.float32)
        moe_sum = moe_sum + jnp.where(chosen[:, None], gate_value[:, None] * returned, 0.0)
        return (moe_sum, position)
    moe_sum = lax.scan(one_expert, jnp.zeros((TOKENS, D), jnp.float32), jnp.arange(EXPERTS, dtype=jnp.int32))[0]
    next_hidden = (flat_hidden + moe_sum).astype(jnp.bfloat16)
    latent_raw = jnp.dot(next_hidden, latent_weight, preferred_element_type=jnp.float32)
    latent_rms = lax.rsqrt(lax.optimization_barrier(jnp.mean(latent_raw * latent_raw, axis=1, keepdims=True)) + norm_eps)
    latent = (latent_raw * latent_rms * latent_gain[None, :]).astype(jnp.bfloat16)
    latent = latent.reshape(TOK_DEV, N_CTX, LATENT).transpose(1, 0, 2).reshape(TOKENS, LATENT)
    prompt_len = PROMPT_BLK * TOK_DEV
    group_len = GROUP_BLK * TOK_DEV
    prompt_keys = latent[:prompt_len]
    prompt_index = jnp.arange(prompt_len, dtype=jnp.int32)
    local_range = jnp.arange(TOK_DEV, dtype=jnp.int32)

    def one_shard(shard_id):
        query_index = (shard_id * TOK_DEV + local_range).astype(jnp.int32)
        group_first = (prompt_len + jnp.maximum(shard_id - PROMPT_BLK, 0) // GROUP_BLK * group_len).astype(jnp.int32)
        group_keys = lax.dynamic_slice_in_dim(latent, group_first, group_len, 0)
        key_block = jnp.concatenate([prompt_keys, group_keys], axis=0).astype(jnp.float32)
        key_index = jnp.concatenate([prompt_index, (group_first + jnp.arange(group_len, dtype=jnp.int32)).astype(jnp.int32)]).astype(jnp.int32)
        key_end = subtree_end[key_index]
        visible = (key_index[None, :] <= query_index[:, None]) & (query_index[:, None] <= key_end[None, :])
        shard_queries = lax.dynamic_slice_in_dim(queries, (shard_id * TOK_DEV).astype(jnp.int32), TOK_DEV, 0).astype(jnp.float32)
        scores = jnp.einsum('qhl,kl->qhk', shard_queries, key_block) * score_scale
        scores = jnp.where(visible[:, None, :], scores, -jnp.inf)
        row_max = lax.optimization_barrier(jnp.max(scores, axis=2, keepdims=True))
        exp_scores = jnp.exp(scores - row_max)
        denom_sum = lax.optimization_barrier(jnp.sum(exp_scores, axis=2))
        weights = lax.optimization_barrier(exp_scores.astype(jnp.bfloat16))
        mixed_sum = jnp.einsum('qhk,kl->qhl', weights.astype(jnp.float32), key_block)
        return (mixed_sum / denom_sum[:, :, None]).astype(jnp.bfloat16)
    attn_out = lax.map(one_shard, jnp.arange(N_CTX, dtype=jnp.int32)).reshape(TOKENS, HEADS, LATENT)
    return (next_hidden.reshape(TOK_DEV, N_CTX, D), attn_out)
```

```python
import jax
import jax.numpy as jnp
from jax import lax
from jax.sharding import PartitionSpec as P

D = 7168
TOP = 8
CAP = 12
GROUPS = 8
BLOCK = 4


score_scale = 192 ** (-0.5)
norm_eps = 1e-06
neg_fill = -1e30


def exchange(chunks, axis):
    return lax.all_to_all(chunks, axis, split_axis=0, concat_axis=0, tiled=True)


def split_two(value):
    high = value.astype(jnp.bfloat16)
    low = (value - high.astype(jnp.float32)).astype(jnp.bfloat16)
    return high, low


def body(
    hidden,
    routes,
    gates,
    moe_gain,
    gate_weight,
    up_weight,
    down_weight,
    latent_weight,
    latent_gain,
    queries,
    subtree_end,
):
    bf16, f32 = jnp.bfloat16, jnp.float32
    row_group, shard_count, width = hidden.shape
    tokens = row_group * shard_count
    exp_count = lax.axis_size("exp")
    ctx_count = lax.axis_size("ctx")
    chips = ctx_count // 2
    slots = exp_count * CAP
    half = slots // 2
    hidden_width = gate_weight.shape[2]
    lanes = hidden_width // chips
    latent_width = latent_weight.shape[1]

    rows = hidden.reshape(tokens, width)
    route_ids = routes.reshape(tokens, TOP)
    route_gates = gates.reshape(tokens, TOP)
    expert_range = jnp.arange(exp_count, dtype=jnp.int32)
    matches = route_ids[:, :, None] == expert_range[None, None, :]
    picked = jnp.sum(matches.astype(f32), axis=1)
    gate_table = jnp.sum(jnp.where(matches, route_gates[:, :, None], 0.0), axis=1)
    earlier = (jnp.arange(tokens)[:, None] < jnp.arange(tokens)[None, :]).astype(bf16)
    rank = jnp.einsum("te,tu->eu", picked.astype(bf16), earlier, preferred_element_type=f32)
    code = jnp.where(picked.T > 0, rank, -1.0)
    placed = code[:, None, :] == jnp.arange(CAP, dtype=f32)[None, :, None]
    placed = placed.reshape(slots, tokens)
    dispatched = jnp.dot(placed.astype(bf16), rows, preferred_element_type=f32).astype(bf16)
    dispatched = jnp.pad(dispatched.reshape(exp_count, CAP, width), ((0, 0), (0, 0), (0, 256 - width)))
    received = exchange(dispatched.reshape(exp_count, 2 * CAP, 128), "exp")
    received = received.reshape(exp_count, CAP, 256)[:, :, :width].reshape(slots, width)

    received_float = received.astype(f32)
    square_part = jnp.sum(received_float * received_float, axis=1)
    scaled = (received_float * moe_gain[None, :]).astype(bf16)
    gate_part = jnp.dot(scaled, gate_weight[0], preferred_element_type=f32).astype(bf16)
    up_part = jnp.dot(scaled, up_weight[0], preferred_element_type=f32).astype(bf16)

    def by_owner(part):
        return part.reshape(2, half, chips, lanes).transpose(2, 0, 1, 3)

    high, low = split_two(square_part.reshape(2, half))
    square_rows = jnp.pad(jnp.stack([high, low], axis=1), ((0, 0), (0, 6), (0, lanes - half)))
    square_rows = jnp.broadcast_to(square_rows[None], (chips,) + square_rows.shape)
    partial = jnp.concatenate([by_owner(gate_part), by_owner(up_part), square_rows], axis=2)
    partial = exchange(partial.reshape(ctx_count, 2 * half + 8, lanes), "ctx")
    total = jnp.sum(partial.astype(f32), axis=0)
    square_total = total[2 * half, :half] + total[2 * half + 1, :half]
    inv_rms = lax.rsqrt(square_total / D + norm_eps)[:, None]
    activated = (jax.nn.silu(total[:half] * inv_rms) * (total[half : 2 * half] * inv_rms)).astype(bf16)
    spread = exchange(jnp.broadcast_to(activated[None], (ctx_count, half, lanes)), "ctx")
    spread = spread.reshape(chips, 2, half, lanes).transpose(1, 2, 0, 3).reshape(slots, hidden_width)
    expert_out = jnp.dot(spread, down_weight[0], preferred_element_type=f32).astype(bf16)

    expert_out = jnp.pad(expert_out.reshape(exp_count, CAP, width), ((0, 0), (0, 0), (0, 256 - width)))
    returned = exchange(expert_out.reshape(exp_count, 2 * CAP, 128), "exp")
    returned = returned.reshape(exp_count, CAP, 256)[:, :, :width].reshape(slots, width)
    gate_high, gate_low = split_two(gate_table.T)

    def weighted(table):
        spread_table = jnp.broadcast_to(table[:, None, :], (exp_count, CAP, tokens)).reshape(slots, tokens)
        return jnp.where(placed, spread_table, jnp.zeros_like(spread_table))

    moe = jnp.einsum("qt,qd->td", weighted(gate_high), returned, preferred_element_type=f32)
    moe += jnp.einsum("qt,qd->td", weighted(gate_low), returned, preferred_element_type=f32)
    next_rows = (rows.astype(f32) + moe).astype(bf16)

    latent_part = jnp.dot(next_rows, latent_weight, preferred_element_type=f32).astype(bf16)
    latent_part = latent_part.reshape(row_group, GROUPS, BLOCK, latent_width).transpose(2, 0, 1, 3)
    latent_part = exchange(latent_part.reshape(ctx_count, GROUPS, latent_width), "ctx")
    latent_raw = jnp.sum(latent_part.astype(f32), axis=0)
    latent_rms = lax.rsqrt(jnp.mean(latent_raw * latent_raw, axis=1, keepdims=True) + norm_eps)
    latent = (latent_raw * latent_rms * latent_gain[None, :]).astype(bf16)
    plane = exchange(jnp.broadcast_to(latent[None], (exp_count,) + latent.shape), "exp")
    plane = plane.transpose(1, 0, 2)
    own = jnp.repeat(plane, BLOCK, axis=0)
    prompt = jnp.broadcast_to(plane[:1], own.shape)
    keys = exchange(jnp.concatenate([prompt, own], axis=1), "ctx")
    keys = keys.reshape(ctx_count * 2 * exp_count, latent_width)

    shard_index = lax.axis_index("ctx")
    group = shard_index // BLOCK
    ends = subtree_end.reshape(GROUPS, BLOCK, exp_count, row_group)
    positions = jnp.arange(subtree_end.shape[0], dtype=jnp.int32).reshape(ends.shape)

    def key_order(table, hide):
        own_table = lax.dynamic_index_in_dim(table, group, 0, keepdims=False)
        own_table = jnp.where(group == 0, hide, own_table)
        both = jnp.stack([table[0], own_table])
        return both.transpose(1, 3, 0, 2).reshape(-1)

    key_end = key_order(ends, -1)
    key_index = key_order(positions, 0)
    local = queries.shape[0]
    heads = queries.shape[1]
    query_index = shard_index * local + jnp.arange(local, dtype=jnp.int32)
    visible = (key_index[None, :] <= query_index[:, None]) & (query_index[:, None] <= key_end[None, :])
    scores = jnp.einsum("qhl,kl->qhk", queries, keys, preferred_element_type=f32) * score_scale
    scores = jnp.where(visible[:, None, :], scores, neg_fill)
    top = jnp.max(scores, axis=2, keepdims=True)
    exp_scores = jnp.where(visible[:, None, :], jnp.exp(scores - top), 0.0)
    denom = jnp.sum(exp_scores, axis=2)
    mixed = jnp.einsum("qhk,kl->qhl", exp_scores.astype(bf16), keys, preferred_element_type=f32)
    attn_out = (mixed / denom[:, :, None]).astype(bf16)
    return (next_rows.reshape(hidden.shape), attn_out)


def solution(mesh):
    return jax.shard_map(
        body,
        mesh=mesh,
        in_specs=(
            P("exp", None, "ctx"),
            P("exp", None, None),
            P("exp", None, None),
            P("ctx"),
            P("exp", "ctx", None),
            P("exp", "ctx", None),
            P("exp", None, "ctx"),
            P("ctx", None),
            P(),
            P("ctx", "exp", None),
            P(),
        ),
        out_specs=(P("exp", None, "ctx"), P("ctx", "exp", None)),
        check_vma=False,
    )
```

```python
import jax
import jax.numpy as jnp
from jax import lax
from jax.experimental import pallas as pl
from jax.experimental.pallas import tpu as pltpu
from jax.sharding import PartitionSpec as P

D = 7168
TOP = 8
CAP = 12
PART = 6
PAD = 8
WIDE = 256
GROUPS = 8
BLOCK = 4
COST = 400_000_000_000


score_scale = 192 ** (-0.5)
norm_eps = 1e-06
neg_fill = -1e30
bf16, f32 = jnp.bfloat16, jnp.float32


def exchange(chunks, axis):
    return lax.all_to_all(chunks, axis, split_axis=0, concat_axis=0, tiled=True)


def exchange_chips(chunks):
    count = lax.axis_size("ctx")
    groups = [list(range(core, count, 2)) for core in range(2)]
    return lax.all_to_all(
        chunks, "ctx", split_axis=0, concat_axis=0, tiled=True, axis_index_groups=groups
    )


def swap(value):
    count = lax.axis_size("ctx")
    return lax.ppermute(value, "ctx", [(i, i ^ 1) for i in range(count)])


def dot(left, right):
    return jnp.dot(left, right, preferred_element_type=f32)


def dot_last(left, right):
    return lax.dot_general(left, right, (((1,), (1,)), ((), ())), preferred_element_type=f32)


def iota(shape, dim):
    return lax.broadcasted_iota(jnp.int32, shape, dim)


def local_kernel(kernel, out_shape, *operands, spaces=None, grant=6, **kwargs):
    spaces = spaces or [pltpu.VMEM] * len(operands)
    return pl.pallas_call(
        kernel,
        out_shape=out_shape,
        in_specs=[pl.BlockSpec(memory_space=space) for space in spaces],
        out_specs=jax.tree.map(lambda _: pl.BlockSpec(memory_space=pltpu.VMEM), out_shape),
        compiler_params=pltpu.CompilerParams(vmem_limit_bytes=grant * 1024 * 1024),
        **kwargs,
    )(*operands)


def routing_kernel(core_ref, expert_ref, gate_ref, placed_ref, table_ref):
    core = core_ref[0]
    group, run = expert_ref.shape
    tokens = group * run
    spread = (iota((tokens, group), 0) // run == iota((tokens, group), 1)).astype(f32)
    inside = iota((tokens, run), 0) % run == iota((tokens, run), 1)

    def column(values):
        values = jnp.dot(spread, values, preferred_element_type=f32, precision=lax.Precision.HIGHEST)
        return jnp.sum(jnp.where(inside, values, 0.0), axis=1, keepdims=True)

    expert, gate = column(expert_ref[...]), column(gate_ref[...])
    lane = iota((tokens, 128), 1).astype(f32)
    picked = expert == lane
    earlier = (iota((tokens, tokens), 1) < iota((tokens, tokens), 0)).astype(bf16)
    rank = dot(earlier, picked.astype(bf16))
    rank = jnp.sum(jnp.where(picked, rank, 0.0), axis=1, keepdims=True)

    def slot_in(part):
        place = rank - (part * PART).astype(f32)
        valid = (expert >= 0) & (place >= 0) & (place < PART)
        return jnp.where(valid, expert * PAD + place, -1.0)

    slot = slot_in(core)
    padded = placed_ref.shape[0]
    slot_rows = jnp.transpose(jnp.broadcast_to(slot, (tokens, padded)))
    placed_ref[...] = (slot_rows == iota((padded, tokens), 0).astype(f32)).astype(bf16)
    table_ref[...] = jnp.where(lane == 0, slot, jnp.where(lane == 1, slot_in(1 - core), gate))


def dispatch_kernel(placed_ref, own_ref, pair_ref, out_ref):
    placed = placed_ref[...]
    width = own_ref.shape[1]
    for start, rows in ((0, own_ref), (WIDE, pair_ref)):
        out_ref[:, start : start + WIDE] = jnp.zeros((placed.shape[0], WIDE), bf16)
        out_ref[:, start : start + width] = dot(placed, rows[...]).astype(bf16)


def slot_choice(rows, columns, half, flip):
    wide, narrow = (1, 0) if not flip else (0, 1)
    padded, packed = iota((rows, columns), wide), iota((rows, columns), narrow)
    packed_place = packed // PART * PAD + packed % PART
    return ((padded == packed_place) & (packed < half)).astype(bf16)


def packed_kernel(half, received_ref, gain_ref, gain_pair_ref, own_ref, pair_ref, square_ref):
    width = gain_ref.shape[1]
    rows = dot(slot_choice(128, received_ref.shape[0], half, False), received_ref[...])
    own_ref[...] = (rows[:half, :width] * gain_ref[0:1, :]).astype(bf16)
    pair_ref[...] = (rows[:half, WIDE : WIDE + width] * gain_pair_ref[0:1, :]).astype(bf16)
    squares = jnp.sum(rows * rows, axis=1, keepdims=True)
    squares = jnp.transpose(jnp.broadcast_to(squares, (128, 128)))[:16]
    high = squares.astype(bf16).astype(f32)
    sub = iota((16, 128), 0)
    square_ref[...] = jnp.where(sub == 0, high, jnp.where(sub == 1, squares - high, 0.0)).astype(bf16)


def gate_up_kernel(own_ref, pair_ref, square_ref, gate_own, gate_pair, up_own, up_pair, out_ref):
    half = own_ref.shape[0]
    owners, _, lanes = out_ref.shape
    own, pair, squares = own_ref[...], pair_ref[...], square_ref[...]
    group = 4
    for first in range(0, owners, group):
        span = slice(first * lanes, (first + group) * lanes)
        gate = (dot(own, gate_own[:, span]) + dot(pair, gate_pair[:, span])).astype(bf16)
        up = (dot(own, up_own[:, span]) + dot(pair, up_pair[:, span])).astype(bf16)
        for at in range(group):
            lane = slice(at * lanes, (at + 1) * lanes)
            out_ref[first + at, :half] = gate[:, lane]
            out_ref[first + at, half : 2 * half] = up[:, lane]
            out_ref[first + at, 2 * half :] = squares


def hidden_unit_kernel(half, partial_ref, out_ref):
    total = jnp.sum(partial_ref[...].astype(f32), axis=0)
    squares = total[2 * half : 2 * half + 1] + total[2 * half + 1 : 2 * half + 2]
    lanes = squares.shape[1]
    scale = lax.rsqrt(squares / D + norm_eps)
    scale = jnp.transpose(jnp.broadcast_to(scale, (lanes, lanes)))[:half]
    gate = total[:half] * scale
    up = total[half : 2 * half] * scale
    units = (gate / (1.0 + jnp.exp(-gate)) * up).astype(bf16)
    for owner in range(out_ref.shape[0]):
        out_ref[owner] = units


def combine_kernel(returned_ref, table_ref, rows_ref, own_ref, pair_ref, out_ref):
    tokens, width = rows_ref.shape
    padded = returned_ref.shape[0]
    slot, gate = table_ref[:, 0:1], table_ref[:, 2:3]
    choice = (slot == iota((tokens, padded), 1).astype(f32)).astype(bf16)
    moe = dot(choice, returned_ref[...]) * gate
    next_own = (rows_ref[...].astype(f32) + moe[:, :width]).astype(bf16)
    next_pair = moe[:, WIDE : WIDE + width].astype(bf16)
    target, source = iota((tokens, tokens), 0), iota((tokens, tokens), 1)
    run = GROUPS * BLOCK
    rest = target % (tokens // BLOCK)
    wanted = rest // GROUPS * run + rest % GROUPS * BLOCK + target // (tokens // BLOCK)
    order = (source == wanted).astype(bf16)
    own = dot(order, next_own).astype(bf16)
    pair = dot(order, next_pair).astype(bf16)
    out_ref[...] = (dot(own, own_ref[...]) + dot(pair, pair_ref[...])).astype(bf16)


def next_kernel(returned_ref, rest_ref, table_ref, rows_ref, out_ref):
    tokens, width = rows_ref.shape
    padded = returned_ref.shape[0]
    lane = iota((tokens, padded), 1).astype(f32)
    moe = dot((table_ref[:, 0:1] == lane).astype(bf16), returned_ref[:, :width])
    moe += dot((table_ref[:, 1:2] == lane).astype(bf16), rest_ref[:, :width])
    out_ref[...] = (rows_ref[...].astype(f32) + moe * table_ref[:, 2:3]).astype(bf16)


def body(
    hidden,
    routes,
    gates,
    moe_gain,
    gate_weight,
    up_weight,
    down_weight,
    latent_weight,
    latent_gain,
    queries,
    subtree_end,
):
    row_group, shard_count, width = hidden.shape
    tokens = row_group * shard_count
    exp_count = lax.axis_size("exp")
    ctx_count = lax.axis_size("ctx")
    chips = ctx_count // 2
    half = exp_count * PART
    padded = exp_count * PAD
    hidden_width = gate_weight.shape[2]
    lanes = hidden_width // chips
    latent_width = latent_weight.shape[1]

    rows = hidden.reshape(tokens, width)
    rows_pair = swap(rows)
    core = lax.rem(lax.axis_index("ctx"), 2)
    shape = jax.ShapeDtypeStruct
    near = routes < exp_count
    expert = jnp.max(jnp.where(near, routes, -1), axis=2).astype(f32)
    gate = jnp.sum(jnp.where(near, gates, 0.0), axis=2)
    placed, table = local_kernel(
        routing_kernel,
        (shape((padded, tokens), bf16), shape((tokens, 128), f32)),
        core.reshape(1),
        expert,
        gate,
        spaces=[pltpu.SMEM] + [pltpu.VMEM] * 2,
    )
    wide = shape((padded, 2 * WIDE), bf16)
    dispatched = local_kernel(dispatch_kernel, wide, placed, rows, rows_pair)
    own = (moe_gain, gate_weight[0], up_weight[0], down_weight[0].T, latent_weight)
    dispatched, own = lax.optimization_barrier((dispatched, own))
    gain_own = jnp.broadcast_to(own[0][None, :], (8, width))
    down_own = own[3]
    gain_pair, gate_pair, up_pair, down_pair, latent_pair = [swap(value) for value in (gain_own,) + own[1:]]
    gate_own, up_own = own[1], own[2]
    received = exchange(dispatched.reshape(exp_count, PAD, 2 * WIDE), "exp").reshape(padded, 2 * WIDE)

    packed = local_kernel(
        lambda *refs: packed_kernel(half, *refs),
        (shape((half, width), bf16), shape((half, width), bf16), shape((16, 128), bf16)),
        received,
        gain_own,
        gain_pair,
        cost_estimate=pl.CostEstimate(flops=COST, bytes_accessed=COST, transcendentals=0),
    )
    partial = local_kernel(
        gate_up_kernel, shape((chips, 2 * half + 16, lanes), bf16), *packed, gate_own, gate_pair, up_own, up_pair
    )
    partial = exchange_chips(partial)
    units = local_kernel(
        lambda *refs: hidden_unit_kernel(half, *refs), shape((chips, half, lanes), bf16), partial
    )
    spread = exchange_chips(units).transpose(1, 0, 2).reshape(half, hidden_width)

    fill = ((0, 0), (0, WIDE - width))
    expert_out = jnp.concatenate(
        [
            jnp.pad(lax.dot_general(spread, w, (((1,), (1,)), ((), ())), preferred_element_type=f32).astype(bf16), fill)
            for w in (down_own, down_pair)
        ],
        axis=1,
    )
    expert_out = jnp.pad(expert_out.reshape(exp_count, PART, 2 * WIDE), ((0, 0), (0, PAD - PART), (0, 0)))
    returned = exchange(expert_out, "exp").reshape(padded, 2 * WIDE)
    returned_rest = swap(returned[:, WIDE:])
    latent_part = local_kernel(
        combine_kernel,
        jax.ShapeDtypeStruct((tokens, latent_width), bf16),
        returned,
        table,
        rows,
        latent_weight,
        latent_pair,
    )
    latent_part = exchange(latent_part.reshape(ctx_count, GROUPS, latent_width), "ctx")
    latent_raw = jnp.sum(latent_part.astype(f32), axis=0)
    latent_rms = lax.rsqrt(jnp.mean(latent_raw * latent_raw, axis=1, keepdims=True) + norm_eps)
    latent = (latent_raw * latent_rms * latent_gain[None, :]).astype(bf16)
    latent, returned_rest = lax.optimization_barrier((latent, returned_rest))
    plane = exchange(jnp.broadcast_to(latent[None], (exp_count,) + latent.shape), "exp")
    plane = plane.transpose(1, 0, 2)
    own = jnp.repeat(plane, BLOCK // 2, axis=0)
    prompt = jnp.broadcast_to(plane[:1], own.shape)
    keys = exchange_chips(jnp.concatenate([prompt, own], axis=1))
    keys = keys.reshape(chips * 2 * exp_count, latent_width)
    all_keys = (keys, swap(keys))

    next_rows = local_kernel(
        next_kernel, jax.ShapeDtypeStruct(rows.shape, bf16), returned, returned_rest, table, rows
    )

    shard_index = lax.axis_index("ctx")
    group = shard_index // BLOCK
    ends = subtree_end.reshape(GROUPS, BLOCK, exp_count, row_group // 2, 2)
    positions = jnp.arange(subtree_end.shape[0], dtype=jnp.int32).reshape(ends.shape)

    def key_order(table, hide, part):
        table = lax.dynamic_index_in_dim(table, part, 4, keepdims=False)
        own_table = lax.dynamic_index_in_dim(table, group, 0, keepdims=False)
        own_table = jnp.where(group == 0, hide, own_table)
        both = jnp.stack([table[0], own_table])
        return both.transpose(1, 3, 0, 2).reshape(-1)

    local, heads = queries.shape[:2]
    query_index = shard_index * local + jnp.arange(local, dtype=jnp.int32)

    def attended(part_keys, part):
        key_end, key_index = key_order(ends, -1, part), key_order(positions, 0, part)
        visible = (key_index[None, :] <= query_index[:, None]) & (query_index[:, None] <= key_end[None, :])
        visible = visible[:, None, :]
        scores = jnp.einsum("qhl,kl->qhk", queries, part_keys, preferred_element_type=f32) * score_scale
        scores = jnp.where(visible, scores, neg_fill)
        top = jnp.max(scores, axis=2)
        exp_scores = jnp.where(visible, jnp.exp(scores - top[:, :, None]), 0.0)
        mixed = jnp.einsum("qhk,kl->qhl", exp_scores.astype(bf16), part_keys, preferred_element_type=f32)
        return top, jnp.sum(exp_scores, axis=2), mixed

    parts = [attended(part_keys, part) for part_keys, part in zip(all_keys, (core, 1 - core))]
    top = jnp.maximum(parts[0][0], parts[1][0])
    shares = [jnp.exp(part[0] - top) for part in parts]
    denom = sum(share * part[1] for share, part in zip(shares, parts))
    mixed = sum(share[:, :, None] * part[2] for share, part in zip(shares, parts))
    attn_out = (mixed / denom[:, :, None]).astype(bf16)
    return (next_rows.reshape(hidden.shape), attn_out)


def solution(mesh):
    return jax.shard_map(
        body,
        mesh=mesh,
        in_specs=(
            P("exp", None, "ctx"),
            P("exp", None, None),
            P("exp", None, None),
            P("ctx"),
            P("exp", "ctx", None),
            P("exp", "ctx", None),
            P("exp", None, "ctx"),
            P("ctx", None),
            P(),
            P("ctx", "exp", None),
            P(),
        ),
        out_specs=(P("exp", None, "ctx"), P("ctx", "exp", None)),
        check_vma=False,
    )
```

```python
import jax
import jax.numpy as jnp
from jax import lax
from jax.experimental import pallas as pl
from jax.experimental.pallas import tpu as pltpu
from jax.sharding import PartitionSpec as P

D = 7168
TOP = 8
CAP = 12
PART = 6
PAD = 8
WIDE = 256
GROUPS = 8
BLOCK = 4
COST = 5_000_000_000


score_scale = 192 ** (-0.5)
norm_eps = 1e-06
neg_fill = -1e30
bf16, f32 = jnp.bfloat16, jnp.float32


def exchange(chunks, axis):
    return lax.all_to_all(chunks, axis, split_axis=0, concat_axis=0, tiled=True)


def exchange_chips(chunks):
    count = lax.axis_size("ctx")
    groups = [list(range(core, count, 2)) for core in range(2)]
    return lax.all_to_all(
        chunks, "ctx", split_axis=0, concat_axis=0, tiled=True, axis_index_groups=groups
    )


def swap(value):
    count = lax.axis_size("ctx")
    return lax.ppermute(value, "ctx", [(i, i ^ 1) for i in range(count)])


def dot(left, right):
    return jnp.dot(left, right, preferred_element_type=f32)


def dot_last(left, right):
    return lax.dot_general(left, right, (((1,), (1,)), ((), ())), preferred_element_type=f32)


def iota(shape, dim):
    return lax.broadcasted_iota(jnp.int32, shape, dim)


def local_kernel(kernel, out_shape, *operands, spaces=None, grant=6, **kwargs):
    spaces = spaces or [pltpu.VMEM] * len(operands)
    return pl.pallas_call(
        kernel,
        out_shape=out_shape,
        in_specs=[pl.BlockSpec(memory_space=space) for space in spaces],
        out_specs=jax.tree.map(lambda _: pl.BlockSpec(memory_space=pltpu.VMEM), out_shape),
        compiler_params=pltpu.CompilerParams(vmem_limit_bytes=grant * 1024 * 1024),
        **kwargs,
    )(*operands)


def column(values):
    group, run = values.shape
    tokens = group * run
    spread = (iota((tokens, group), 0) // run == iota((tokens, group), 1)).astype(f32)
    inside = iota((tokens, run), 0) % run == iota((tokens, run), 1)
    values = jnp.dot(spread, values, preferred_element_type=f32, precision=lax.Precision.HIGHEST)
    return jnp.sum(jnp.where(inside, values, 0.0), axis=1, keepdims=True)


def gate_kernel(gate_ref, gain_ref, out_ref, gains_ref):
    out_ref[...] = jnp.broadcast_to(column(gate_ref[...]), out_ref.shape)
    gains_ref[...] = jnp.broadcast_to(gain_ref[...], gains_ref.shape)


def routing_kernel(core_ref, expert_ref, placed_ref, table_ref):
    core = core_ref[0]
    expert = column(expert_ref[...])
    tokens = expert.shape[0]
    lane = iota((tokens, 128), 1).astype(f32)
    picked = expert == lane
    earlier = (iota((tokens, tokens), 1) < iota((tokens, tokens), 0)).astype(bf16)
    rank = dot(earlier, picked.astype(bf16))
    rank = jnp.sum(jnp.where(picked, rank, 0.0), axis=1, keepdims=True)

    def slot_in(part):
        place = rank - (part * PART).astype(f32)
        valid = (expert >= 0) & (place >= 0) & (place < PART)
        return jnp.where(valid, expert * PAD + place, -1.0)

    slot = slot_in(core)
    padded = placed_ref.shape[0]
    slot_rows = jnp.transpose(jnp.broadcast_to(slot, (tokens, padded)))
    placed_ref[...] = (slot_rows == iota((padded, tokens), 0).astype(f32)).astype(bf16)
    table_ref[...] = jnp.where(lane == 0, slot, slot_in(1 - core))


def dispatch_kernel(placed_ref, own_ref, pair_ref, out_ref):
    placed = placed_ref[...]
    width = own_ref.shape[1]
    for start, rows in ((0, own_ref), (WIDE, pair_ref)):
        out_ref[:, start : start + WIDE] = jnp.zeros((placed.shape[0], WIDE), bf16)
        out_ref[:, start : start + width] = dot(placed, rows[...]).astype(bf16)


def slot_choice(rows, columns, half, flip):
    wide, narrow = (1, 0) if not flip else (0, 1)
    padded, packed = iota((rows, columns), wide), iota((rows, columns), narrow)
    packed_place = packed // PART * PAD + packed % PART
    return ((padded == packed_place) & (packed < half)).astype(bf16)


def packed_kernel(half, received_ref, gain_ref, gain_pair_ref, own_ref, pair_ref, square_ref):
    width = gain_ref.shape[1]
    rows = dot(slot_choice(128, received_ref.shape[0], half, False), received_ref[...])
    own_ref[...] = (rows[:half, :width] * gain_ref[0:1, :]).astype(bf16)
    pair_ref[...] = (rows[:half, WIDE : WIDE + width] * gain_pair_ref[0:1, :]).astype(bf16)
    squares = jnp.sum(rows * rows, axis=1, keepdims=True)
    squares = jnp.transpose(jnp.broadcast_to(squares, (128, 128)))[:16]
    high = squares.astype(bf16).astype(f32)
    sub = iota((16, 128), 0)
    square_ref[...] = jnp.where(sub == 0, high, jnp.where(sub == 1, squares - high, 0.0)).astype(bf16)


def gate_up_kernel(own_ref, pair_ref, square_ref, gate_own, gate_pair, up_own, up_pair, out_ref):
    half = own_ref.shape[0]
    owners, _, lanes = out_ref.shape
    own, pair, squares = own_ref[...], pair_ref[...], square_ref[...]
    group = 4
    for first in range(0, owners, group):
        span = slice(first * lanes, (first + group) * lanes)
        gate = (dot(own, gate_own[:, span]) + dot(pair, gate_pair[:, span])).astype(bf16)
        up = (dot(own, up_own[:, span]) + dot(pair, up_pair[:, span])).astype(bf16)
        for at in range(group):
            lane = slice(at * lanes, (at + 1) * lanes)
            out_ref[first + at, :half] = gate[:, lane]
            out_ref[first + at, half : 2 * half] = up[:, lane]
            out_ref[first + at, 2 * half :] = squares


def hidden_unit_kernel(half, partial_ref, out_ref):
    total = jnp.sum(partial_ref[...].astype(f32), axis=0)
    squares = total[2 * half : 2 * half + 1] + total[2 * half + 1 : 2 * half + 2]
    lanes = squares.shape[1]
    scale = lax.rsqrt(squares / D + norm_eps)
    scale = jnp.transpose(jnp.broadcast_to(scale, (lanes, lanes)))[:half]
    gate = total[:half] * scale
    up = total[half : 2 * half] * scale
    units = (gate / (1.0 + jnp.exp(-gate)) * up).astype(bf16)
    for owner in range(out_ref.shape[0]):
        out_ref[owner] = units


def combine_kernel(returned_ref, table_ref, gate_ref, rows_ref, own_ref, pair_ref, out_ref):
    tokens, width = rows_ref.shape
    padded = returned_ref.shape[0]
    slot, gate = table_ref[:, 0:1], gate_ref[:, 0:1]
    choice = (slot == iota((tokens, padded), 1).astype(f32)).astype(bf16)
    moe = dot(choice, returned_ref[...]) * gate
    next_own = (rows_ref[...].astype(f32) + moe[:, :width]).astype(bf16)
    next_pair = moe[:, WIDE : WIDE + width].astype(bf16)
    target, source = iota((tokens, tokens), 0), iota((tokens, tokens), 1)
    run = GROUPS * BLOCK
    rest = target % (tokens // BLOCK)
    wanted = rest // GROUPS * run + rest % GROUPS * BLOCK + target // (tokens // BLOCK)
    order = (source == wanted).astype(bf16)
    own = dot(order, next_own).astype(bf16)
    pair = dot(order, next_pair).astype(bf16)
    out_ref[...] = (dot(own, own_ref[...]) + dot(pair, pair_ref[...])).astype(bf16)


def latent_kernel(part_ref, gain_ref, out_ref):
    raw = jnp.sum(part_ref[...].astype(f32), axis=0)
    scale = lax.rsqrt(jnp.mean(raw * raw, axis=1, keepdims=True) + norm_eps)
    latent = (raw * scale * gain_ref[...]).astype(bf16)
    for plane in range(out_ref.shape[0]):
        out_ref[plane] = latent


def key_kernel(plane_ref, out_ref):
    chips, rows, _ = out_ref.shape
    planes = rows // 2
    total = plane_ref.shape[0]
    target, source = iota((total, total), 0), iota((total, total), 1)
    order = (source == target % planes * GROUPS + target // planes).astype(bf16)
    ordered = dot(order, plane_ref[...]).astype(bf16)
    for chip in range(chips):
        run = chip // (BLOCK // 2)
        out_ref[chip, :planes] = ordered[:planes]
        out_ref[chip, planes:] = ordered[run * planes : (run + 1) * planes]


def next_kernel(returned_ref, rest_ref, table_ref, gate_ref, rows_ref, out_ref):
    tokens, width = rows_ref.shape
    padded = returned_ref.shape[0]
    lane = iota((tokens, padded), 1).astype(f32)
    moe = dot((table_ref[:, 0:1] == lane).astype(bf16), returned_ref[:, :width])
    moe += dot((table_ref[:, 1:2] == lane).astype(bf16), rest_ref[:, :width])
    out_ref[...] = (rows_ref[...].astype(f32) + moe * gate_ref[:, 0:1]).astype(bf16)


def attend(queries_ref, keys_ref, seen_ref):
    keys = keys_ref[...]
    seen = jnp.concatenate([seen_ref[...]] * (queries_ref.shape[0] // seen_ref.shape[0]), axis=0) > 0
    scores = jnp.where(seen, dot_last(queries_ref[...], keys) * score_scale, neg_fill)
    top = jnp.max(scores, axis=1, keepdims=True)
    weights = jnp.where(seen, jnp.exp(scores - top), 0.0)
    return top, jnp.sum(weights, axis=1, keepdims=True), dot(weights.astype(bf16), keys)


def first_kernel(queries_ref, keys_ref, seen_ref, stats_ref, mixed_ref):
    top, denom, mixed = attend(queries_ref, keys_ref, seen_ref)
    stats_ref[...] = jnp.where(iota(stats_ref.shape, 1) == 0, top, denom)
    mixed_ref[...] = mixed


def second_kernel(queries_ref, keys_ref, seen_ref, stats_ref, mixed_ref, out_ref):
    top, denom, mixed = attend(queries_ref, keys_ref, seen_ref)
    first_top, first_denom = stats_ref[:, 0:1], stats_ref[:, 1:2]
    most = jnp.maximum(top, first_top)
    share, first_share = jnp.exp(top - most), jnp.exp(first_top - most)
    total = denom * share + first_denom * first_share
    out_ref[...] = (mixed * (share / total) + mixed_ref[...] * (first_share / total)).astype(bf16)


def body(
    hidden,
    routes,
    gates,
    moe_gain,
    gate_weight,
    up_weight,
    down_weight,
    latent_weight,
    latent_gain,
    queries,
    subtree_end,
):
    row_group, shard_count, width = hidden.shape
    tokens = row_group * shard_count
    exp_count = lax.axis_size("exp")
    ctx_count = lax.axis_size("ctx")
    chips = ctx_count // 2
    half = exp_count * PART
    padded = exp_count * PAD
    hidden_width = gate_weight.shape[2]
    lanes = hidden_width // chips
    latent_width = latent_weight.shape[1]

    rows = hidden.reshape(tokens, width)
    rows_pair = swap(rows)
    core = lax.rem(lax.axis_index("ctx"), 2)

    shape = jax.ShapeDtypeStruct
    near = routes < exp_count
    expert = jnp.max(jnp.where(near, routes, -1), axis=2).astype(f32)
    placed, table = local_kernel(
        routing_kernel,
        (shape((padded, tokens), bf16), shape((tokens, 128), f32)),
        core.reshape(1),
        expert,
        spaces=[pltpu.SMEM, pltpu.VMEM],
    )
    wide = shape((padded, 2 * WIDE), bf16)
    dispatched = local_kernel(dispatch_kernel, wide, placed, rows, rows_pair)
    own = (gate_weight[0], up_weight[0], down_weight[0].T, latent_weight, moe_gain)
    late = (gates, latent_gain)
    dispatched, own, late = lax.optimization_barrier((dispatched, own, late))
    gate = jnp.sum(jnp.where(near, late[0], 0.0), axis=2)
    gate, latent_gains = local_kernel(
        gate_kernel, (shape((tokens, 128), f32), shape((8, latent_width), f32)), gate, late[1][None, :]
    )
    gate_own, up_own, down_own, _, gain_own = own
    gain_own = jnp.broadcast_to(gain_own[None, :], (8, width))
    gate_pair, up_pair, down_pair, latent_pair, gain_pair = [swap(value) for value in own[:4] + (gain_own,)]
    received = exchange(dispatched.reshape(exp_count, PAD, 2 * WIDE), "exp").reshape(padded, 2 * WIDE)

    packed = local_kernel(
        lambda *refs: packed_kernel(half, *refs),
        (shape((half, width), bf16), shape((half, width), bf16), shape((16, 128), bf16)),
        received,
        gain_own,
        gain_pair,
        cost_estimate=pl.CostEstimate(flops=COST, bytes_accessed=COST, transcendentals=0),
    )
    partial = local_kernel(
        gate_up_kernel, shape((chips, 2 * half + 16, lanes), bf16), *packed, gate_own, gate_pair, up_own, up_pair
    )
    partial = exchange_chips(partial)
    units = local_kernel(
        lambda *refs: hidden_unit_kernel(half, *refs), shape((chips, half, lanes), bf16), partial
    )
    spread = exchange_chips(units).transpose(1, 0, 2).reshape(half, hidden_width)

    fill = ((0, 0), (0, WIDE - width))
    expert_out = jnp.concatenate(
        [
            jnp.pad(lax.dot_general(spread, w, (((1,), (1,)), ((), ())), preferred_element_type=f32).astype(bf16), fill)
            for w in (down_own, down_pair)
        ],
        axis=1,
    )
    expert_out = jnp.pad(expert_out.reshape(exp_count, PART, 2 * WIDE), ((0, 0), (0, PAD - PART), (0, 0)))
    returned = exchange(expert_out, "exp").reshape(padded, 2 * WIDE)
    returned_rest = swap(returned[:, WIDE:])
    latent_part = local_kernel(
        combine_kernel,
        jax.ShapeDtypeStruct((tokens, latent_width), bf16),
        returned,
        table,
        gate,
        rows,
        latent_weight,
        latent_pair,
    )
    latent_part = exchange(latent_part.reshape(ctx_count, GROUPS, latent_width), "ctx")
    latent = local_kernel(
        latent_kernel, shape((exp_count, GROUPS, latent_width), bf16), latent_part, latent_gains
    )
    latent, returned_rest = lax.optimization_barrier((latent, returned_rest))
    plane = exchange(latent, "exp").reshape(exp_count * GROUPS, latent_width)
    next_rows = local_kernel(
        next_kernel, shape(rows.shape, bf16), returned, returned_rest, table, gate, rows
    )
    local, heads = queries.shape[:2]
    queries = queries.transpose(1, 0, 2).reshape(heads * local, latent_width)
    chunks = local_kernel(key_kernel, shape((chips, 2 * exp_count, latent_width), bf16), plane)
    chunks, next_rows, queries = lax.optimization_barrier((chunks, next_rows, queries))
    keys = exchange_chips(chunks).reshape(chips * 2 * exp_count, latent_width)
    keys_pair = swap(keys)

    shard_index = lax.axis_index("ctx")
    group = shard_index // BLOCK
    ends = subtree_end.reshape(GROUPS, BLOCK, exp_count, row_group // 2, 2)
    positions = jnp.arange(subtree_end.shape[0], dtype=jnp.int32).reshape(ends.shape)

    def key_order(table, hide, part):
        table = lax.dynamic_index_in_dim(table, part, 4, keepdims=False)
        own_table = lax.dynamic_index_in_dim(table, group, 0, keepdims=False)
        own_table = jnp.where(group == 0, hide, own_table)
        both = jnp.stack([table[0], own_table])
        return both.transpose(1, 3, 0, 2).reshape(-1)

    query_index = shard_index * local + jnp.arange(local, dtype=jnp.int32)

    def visible(part):
        key_end, key_index = key_order(ends, -1, part), key_order(positions, 0, part)
        seen = (key_index[None, :] <= query_index[:, None]) & (query_index[:, None] <= key_end[None, :])
        return seen.astype(f32)

    first = local_kernel(
        first_kernel,
        (shape((heads * local, 128), f32), shape((heads * local, latent_width), f32)),
        queries,
        keys,
        visible(core),
        grant=16,
    )
    attn_out = local_kernel(
        second_kernel,
        shape((heads * local, latent_width), bf16),
        queries,
        keys_pair,
        visible(1 - core),
        *first,
        grant=16,
    )
    attn_out = attn_out.reshape(heads, local, latent_width).transpose(1, 0, 2)
    return (next_rows.reshape(hidden.shape), attn_out)


def solution(mesh):
    return jax.shard_map(
        body,
        mesh=mesh,
        in_specs=(
            P("exp", None, "ctx"),
            P("exp", None, None),
            P("exp", None, None),
            P("ctx"),
            P("exp", "ctx", None),
            P("exp", "ctx", None),
            P("exp", None, "ctx"),
            P("ctx", None),
            P(),
            P("ctx", "exp", None),
            P(),
        ),
        out_specs=(P("exp", None, "ctx"), P("ctx", "exp", None)),
        check_vma=False,
    )
```

```python
import jax
import jax.numpy as jnp
from jax import lax
from jax.experimental import pallas as pl
from jax.experimental.pallas import tpu as pltpu
from jax.sharding import PartitionSpec as P

D = 7168
TOP = 8
CAP = 12
PART = 6
PAD = 8
WIDE = 256
GROUPS = 8
BLOCK = 4
COST = 5_000_000_000


score_scale = 192 ** (-0.5)
norm_eps = 1e-06
neg_fill = -1e30
bf16, f32 = jnp.bfloat16, jnp.float32


def exchange(chunks, axis):
    return lax.all_to_all(chunks, axis, split_axis=0, concat_axis=0, tiled=True)


def exchange_chips(chunks):
    count = lax.axis_size("ctx")
    groups = [list(range(core, count, 2)) for core in range(2)]
    return lax.all_to_all(
        chunks, "ctx", split_axis=0, concat_axis=0, tiled=True, axis_index_groups=groups
    )


def swap(value):
    count = lax.axis_size("ctx")
    return lax.ppermute(value, "ctx", [(i, i ^ 1) for i in range(count)])


def dot(left, right):
    return jnp.dot(left, right, preferred_element_type=f32)


def dot_last(left, right):
    return lax.dot_general(left, right, (((1,), (1,)), ((), ())), preferred_element_type=f32)


def iota(shape, dim):
    return lax.broadcasted_iota(jnp.int32, shape, dim)


def local_kernel(kernel, out_shape, *operands, spaces=None, grant=6, **kwargs):
    spaces = spaces or [pltpu.VMEM] * len(operands)
    return pl.pallas_call(
        kernel,
        out_shape=out_shape,
        in_specs=[pl.BlockSpec(memory_space=space) for space in spaces],
        out_specs=jax.tree.map(lambda _: pl.BlockSpec(memory_space=pltpu.VMEM), out_shape),
        compiler_params=pltpu.CompilerParams(vmem_limit_bytes=grant * 1024 * 1024),
        **kwargs,
    )(*operands)


def column(values):
    group, run = values.shape
    tokens = group * run
    spread = (iota((tokens, group), 0) // run == iota((tokens, group), 1)).astype(f32)
    inside = iota((tokens, run), 0) % run == iota((tokens, run), 1)
    values = jnp.dot(spread, values, preferred_element_type=f32, precision=lax.Precision.HIGHEST)
    return jnp.sum(jnp.where(inside, values, 0.0), axis=1, keepdims=True)


def side_kernel(place_ref, gate_ref, gain_ref, ends_ref, out_ref, gains_ref, seen_ref, seen_pair_ref):
    out_ref[...] = jnp.broadcast_to(column(gate_ref[...]), out_ref.shape)
    gains_ref[...] = jnp.broadcast_to(gain_ref[...], gains_ref.shape)
    shard, core = place_ref[0], place_ref[1]
    local, count = seen_ref.shape
    shards = ends_ref.shape[0]
    ends = ends_ref[...].astype(f32)
    query = (shard * local + iota((local, count), 0)).astype(f32)
    planes = local // 8
    chip, rest = iota((count, 1), 0) // (2 * planes), iota((count, 1), 0) % (2 * planes)
    run = jnp.where(rest >= planes, shard // BLOCK, 0)
    hidden = (rest >= planes) & (shard // BLOCK == 0)
    key_shard = run * BLOCK + chip // 4
    chosen = (iota((count, shards), 1) == key_shard).astype(f32)
    chosen = jnp.dot(chosen, ends, preferred_element_type=f32, precision=lax.Precision.HIGHEST)
    for part, ref in ((core, seen_ref), (1 - core, seen_pair_ref)):
        row = rest % planes * 8 + chip % 4 * 2 + part
        end = jnp.sum(jnp.where(iota((count, local), 1) == row, chosen, 0.0), axis=1, keepdims=True)
        end = jnp.where(hidden, -1.0, end)
        index = (key_shard * local + row).astype(f32)
        end = jnp.transpose(jnp.broadcast_to(end, (count, local)))
        index = jnp.transpose(jnp.broadcast_to(index, (count, local)))
        ref[...] = ((index <= query) & (query <= end)).astype(f32)


def routing_kernel(core_ref, expert_ref, placed_ref, table_ref):
    core = core_ref[0]
    expert = column(expert_ref[...])
    tokens = expert.shape[0]
    lane = iota((tokens, 128), 1).astype(f32)
    picked = expert == lane
    earlier = (iota((tokens, tokens), 1) < iota((tokens, tokens), 0)).astype(bf16)
    rank = dot(earlier, picked.astype(bf16))
    rank = jnp.sum(jnp.where(picked, rank, 0.0), axis=1, keepdims=True)

    def slot_in(part):
        place = rank - (part * PART).astype(f32)
        valid = (expert >= 0) & (place >= 0) & (place < PART)
        return jnp.where(valid, expert * PAD + place, -1.0)

    slot = slot_in(core)
    padded = placed_ref.shape[0]
    slot_rows = jnp.transpose(jnp.broadcast_to(slot, (tokens, padded)))
    placed_ref[...] = (slot_rows == iota((padded, tokens), 0).astype(f32)).astype(bf16)
    table_ref[...] = jnp.where(lane == 0, slot, slot_in(1 - core))


def dispatch_kernel(placed_ref, own_ref, pair_ref, out_ref):
    placed = placed_ref[...]
    width = own_ref.shape[1]
    for start, rows in ((0, own_ref), (WIDE, pair_ref)):
        out_ref[:, start : start + WIDE] = jnp.zeros((placed.shape[0], WIDE), bf16)
        out_ref[:, start : start + width] = dot(placed, rows[...]).astype(bf16)


def slot_choice(rows, columns, half, flip):
    wide, narrow = (1, 0) if not flip else (0, 1)
    padded, packed = iota((rows, columns), wide), iota((rows, columns), narrow)
    packed_place = packed // PART * PAD + packed % PART
    return ((padded == packed_place) & (packed < half)).astype(bf16)


def packed_kernel(half, received_ref, gain_ref, gain_pair_ref, own_ref, pair_ref, square_ref):
    width = gain_ref.shape[1]
    rows = dot(slot_choice(128, received_ref.shape[0], half, False), received_ref[...])
    own_ref[...] = (rows[:half, :width] * gain_ref[0:1, :]).astype(bf16)
    pair_ref[...] = (rows[:half, WIDE : WIDE + width] * gain_pair_ref[0:1, :]).astype(bf16)
    squares = jnp.sum(rows * rows, axis=1, keepdims=True)
    squares = jnp.transpose(jnp.broadcast_to(squares, (128, 128)))[:16]
    high = squares.astype(bf16).astype(f32)
    sub = iota((16, 128), 0)
    square_ref[...] = jnp.where(sub == 0, high, jnp.where(sub == 1, squares - high, 0.0)).astype(bf16)


def gate_up_kernel(own_ref, pair_ref, square_ref, gate_own, gate_pair, up_own, up_pair, out_ref):
    half = own_ref.shape[0]
    owners, _, lanes = out_ref.shape
    own, pair, squares = own_ref[...], pair_ref[...], square_ref[...]
    group = 4
    for first in range(0, owners, group):
        span = slice(first * lanes, (first + group) * lanes)
        gate = (dot(own, gate_own[:, span]) + dot(pair, gate_pair[:, span])).astype(bf16)
        up = (dot(own, up_own[:, span]) + dot(pair, up_pair[:, span])).astype(bf16)
        for at in range(group):
            lane = slice(at * lanes, (at + 1) * lanes)
            out_ref[first + at, :half] = gate[:, lane]
            out_ref[first + at, half : 2 * half] = up[:, lane]
            out_ref[first + at, 2 * half :] = squares


def hidden_unit_kernel(half, partial_ref, out_ref):
    total = jnp.sum(partial_ref[...].astype(f32), axis=0)
    squares = total[2 * half : 2 * half + 1] + total[2 * half + 1 : 2 * half + 2]
    lanes = squares.shape[1]
    scale = lax.rsqrt(squares / D + norm_eps)
    scale = jnp.transpose(jnp.broadcast_to(scale, (lanes, lanes)))[:half]
    gate = total[:half] * scale
    up = total[half : 2 * half] * scale
    units = (gate / (1.0 + jnp.exp(-gate)) * up).astype(bf16)
    for owner in range(out_ref.shape[0]):
        out_ref[owner] = units


def combine_kernel(returned_ref, table_ref, gate_ref, rows_ref, own_ref, pair_ref, out_ref):
    tokens, width = rows_ref.shape
    padded = returned_ref.shape[0]
    slot, gate = table_ref[:, 0:1], gate_ref[:, 0:1]
    choice = (slot == iota((tokens, padded), 1).astype(f32)).astype(bf16)
    moe = dot(choice, returned_ref[...]) * gate
    next_own = (rows_ref[...].astype(f32) + moe[:, :width]).astype(bf16)
    next_pair = moe[:, WIDE : WIDE + width].astype(bf16)
    target, source = iota((tokens, tokens), 0), iota((tokens, tokens), 1)
    run = GROUPS * BLOCK
    rest = target % (tokens // BLOCK)
    wanted = rest // GROUPS * run + rest % GROUPS * BLOCK + target // (tokens // BLOCK)
    order = (source == wanted).astype(bf16)
    own = dot(order, next_own).astype(bf16)
    pair = dot(order, next_pair).astype(bf16)
    out_ref[...] = (dot(own, own_ref[...]) + dot(pair, pair_ref[...])).astype(bf16)


def latent_kernel(part_ref, gain_ref, out_ref):
    raw = jnp.sum(part_ref[...].astype(f32), axis=0)
    scale = lax.rsqrt(jnp.mean(raw * raw, axis=1, keepdims=True) + norm_eps)
    latent = (raw * scale * gain_ref[...]).astype(bf16)
    for plane in range(out_ref.shape[0]):
        out_ref[plane] = latent


def key_kernel(plane_ref, out_ref):
    chips, rows, _ = out_ref.shape
    planes = rows // 2
    total = plane_ref.shape[0]
    target, source = iota((total, total), 0), iota((total, total), 1)
    order = (source == target % planes * GROUPS + target // planes).astype(bf16)
    ordered = dot(order, plane_ref[...]).astype(bf16)
    for chip in range(chips):
        run = chip // (BLOCK // 2)
        out_ref[chip, :planes] = ordered[:planes]
        out_ref[chip, planes:] = ordered[run * planes : (run + 1) * planes]


def next_kernel(returned_ref, rest_ref, table_ref, gate_ref, rows_ref, out_ref):
    tokens, width = rows_ref.shape
    padded = returned_ref.shape[0]
    lane = iota((tokens, padded), 1).astype(f32)
    moe = dot((table_ref[:, 0:1] == lane).astype(bf16), returned_ref[:, :width])
    moe += dot((table_ref[:, 1:2] == lane).astype(bf16), rest_ref[:, :width])
    out_ref[...] = (rows_ref[...].astype(f32) + moe * gate_ref[:, 0:1]).astype(bf16)


def attend(queries_ref, keys_ref, seen_ref):
    keys = keys_ref[...]
    seen = jnp.concatenate([seen_ref[...]] * (queries_ref.shape[0] // seen_ref.shape[0]), axis=0) > 0
    scores = jnp.where(seen, dot_last(queries_ref[...], keys) * score_scale, neg_fill)
    top = jnp.max(scores, axis=1, keepdims=True)
    weights = jnp.where(seen, jnp.exp(scores - top), 0.0)
    return top, jnp.sum(weights, axis=1, keepdims=True), dot(weights.astype(bf16), keys)


def first_kernel(queries_ref, keys_ref, seen_ref, stats_ref, mixed_ref):
    top, denom, mixed = attend(queries_ref, keys_ref, seen_ref)
    stats_ref[...] = jnp.where(iota(stats_ref.shape, 1) == 0, top, denom)
    mixed_ref[...] = mixed


def second_kernel(queries_ref, keys_ref, seen_ref, stats_ref, mixed_ref, out_ref):
    top, denom, mixed = attend(queries_ref, keys_ref, seen_ref)
    first_top, first_denom = stats_ref[:, 0:1], stats_ref[:, 1:2]
    most = jnp.maximum(top, first_top)
    share, first_share = jnp.exp(top - most), jnp.exp(first_top - most)
    total = denom * share + first_denom * first_share
    out_ref[...] = (mixed * (share / total) + mixed_ref[...] * (first_share / total)).astype(bf16)


def body(
    hidden,
    routes,
    gates,
    moe_gain,
    gate_weight,
    up_weight,
    down_weight,
    latent_weight,
    latent_gain,
    queries,
    subtree_end,
):
    row_group, shard_count, width = hidden.shape
    tokens = row_group * shard_count
    exp_count = lax.axis_size("exp")
    ctx_count = lax.axis_size("ctx")
    chips = ctx_count // 2
    half = exp_count * PART
    padded = exp_count * PAD
    hidden_width = gate_weight.shape[2]
    lanes = hidden_width // chips
    latent_width = latent_weight.shape[1]

    rows = hidden.reshape(tokens, width)
    rows_pair = swap(rows)
    core = lax.rem(lax.axis_index("ctx"), 2)

    shape = jax.ShapeDtypeStruct
    near = routes < exp_count
    expert = jnp.max(jnp.where(near, routes, -1), axis=2).astype(f32)
    placed, table = local_kernel(
        routing_kernel,
        (shape((padded, tokens), bf16), shape((tokens, 128), f32)),
        core.reshape(1),
        expert,
        spaces=[pltpu.SMEM, pltpu.VMEM],
    )
    wide = shape((padded, 2 * WIDE), bf16)
    dispatched = local_kernel(dispatch_kernel, wide, placed, rows, rows_pair)
    own = (gate_weight[0], up_weight[0], down_weight[0].T, latent_weight, moe_gain)
    late = (gates, latent_gain, subtree_end)
    dispatched, own, late = lax.optimization_barrier((dispatched, own, late))
    gate = jnp.sum(jnp.where(near, late[0], 0.0), axis=2)
    local, heads = queries.shape[:2]
    sight = shape((local, chips * 2 * exp_count), f32)
    gate, latent_gains, seen, seen_pair = local_kernel(
        side_kernel,
        (shape((tokens, 128), f32), shape((8, latent_width), f32), sight, sight),
        jnp.stack([lax.axis_index("ctx"), core]),
        gate,
        late[1][None, :],
        late[2].reshape(ctx_count, local),
        spaces=[pltpu.SMEM] + [pltpu.VMEM] * 3,
    )
    gate_own, up_own, down_own, _, gain_own = own
    gain_own = jnp.broadcast_to(gain_own[None, :], (8, width))
    gate_pair, up_pair, down_pair, latent_pair, gain_pair = [swap(value) for value in own[:4] + (gain_own,)]
    received = exchange(dispatched.reshape(exp_count, PAD, 2 * WIDE), "exp").reshape(padded, 2 * WIDE)

    packed = local_kernel(
        lambda *refs: packed_kernel(half, *refs),
        (shape((half, width), bf16), shape((half, width), bf16), shape((16, 128), bf16)),
        received,
        gain_own,
        gain_pair,
        cost_estimate=pl.CostEstimate(flops=COST, bytes_accessed=COST, transcendentals=0),
    )
    partial = local_kernel(
        gate_up_kernel, shape((chips, 2 * half + 16, lanes), bf16), *packed, gate_own, gate_pair, up_own, up_pair
    )
    partial = exchange_chips(partial)
    units = local_kernel(
        lambda *refs: hidden_unit_kernel(half, *refs), shape((chips, half, lanes), bf16), partial
    )
    spread = exchange_chips(units).transpose(1, 0, 2).reshape(half, hidden_width)

    fill = ((0, 0), (0, WIDE - width))
    expert_out = jnp.concatenate(
        [
            jnp.pad(lax.dot_general(spread, w, (((1,), (1,)), ((), ())), preferred_element_type=f32).astype(bf16), fill)
            for w in (down_own, down_pair)
        ],
        axis=1,
    )
    expert_out = jnp.pad(expert_out.reshape(exp_count, PART, 2 * WIDE), ((0, 0), (0, PAD - PART), (0, 0)))
    returned = exchange(expert_out, "exp").reshape(padded, 2 * WIDE)
    returned_rest = swap(returned[:, WIDE:])
    latent_part = local_kernel(
        combine_kernel,
        jax.ShapeDtypeStruct((tokens, latent_width), bf16),
        returned,
        table,
        gate,
        rows,
        latent_weight,
        latent_pair,
    )
    latent_part = exchange(latent_part.reshape(ctx_count, GROUPS, latent_width), "ctx")
    latent = local_kernel(
        latent_kernel, shape((exp_count, GROUPS, latent_width), bf16), latent_part, latent_gains
    )
    latent, returned_rest = lax.optimization_barrier((latent, returned_rest))
    plane = exchange(latent, "exp").reshape(exp_count * GROUPS, latent_width)
    next_rows = local_kernel(
        next_kernel, shape(rows.shape, bf16), returned, returned_rest, table, gate, rows
    )
    queries = queries.transpose(1, 0, 2).reshape(heads * local, latent_width)
    chunks = local_kernel(key_kernel, shape((chips, 2 * exp_count, latent_width), bf16), plane)
    chunks, next_rows, queries = lax.optimization_barrier((chunks, next_rows, queries))
    keys = exchange_chips(chunks).reshape(chips * 2 * exp_count, latent_width)
    keys_pair = swap(keys)

    first = local_kernel(
        first_kernel,
        (shape((heads * local, 128), f32), shape((heads * local, latent_width), f32)),
        queries,
        keys,
        seen,
        grant=16,
    )
    attn_out = local_kernel(
        second_kernel,
        shape((heads * local, latent_width), bf16),
        queries,
        keys_pair,
        seen_pair,
        *first,
        grant=16,
    )
    attn_out = attn_out.reshape(heads, local, latent_width).transpose(1, 0, 2)
    return (next_rows.reshape(hidden.shape), attn_out)


def solution(mesh):
    return jax.shard_map(
        body,
        mesh=mesh,
        in_specs=(
            P("exp", None, "ctx"),
            P("exp", None, None),
            P("exp", None, None),
            P("ctx"),
            P("exp", "ctx", None),
            P("exp", "ctx", None),
            P("exp", None, "ctx"),
            P("ctx", None),
            P(),
            P("ctx", "exp", None),
            P(),
        ),
        out_specs=(P("exp", None, "ctx"), P("ctx", "exp", None)),
        check_vma=False,
    )
```

```python
import jax
import jax.numpy as jnp
from jax import lax
from jax.experimental import pallas as pl
from jax.experimental.pallas import tpu as pltpu
from jax.sharding import PartitionSpec as P

D = 7168
TOP = 8
CAP = 12
PART = 6
PAD = 8
WIDE = 256
GROUPS = 8
BLOCK = 4
COST = 5_000_000_000


score_scale = 192 ** (-0.5)
norm_eps = 1e-06
neg_fill = -1e30
bf16, f32 = jnp.bfloat16, jnp.float32


def exchange(chunks, axis):
    return lax.all_to_all(chunks, axis, split_axis=0, concat_axis=0, tiled=True)


def exchange_chips(chunks):
    count = lax.axis_size("ctx")
    groups = [list(range(core, count, 2)) for core in range(2)]
    return lax.all_to_all(
        chunks, "ctx", split_axis=0, concat_axis=0, tiled=True, axis_index_groups=groups
    )


def exchange_pairs(chunks):
    count, planes = lax.axis_size("ctx"), lax.axis_size("exp")
    groups = [list(range(chip * 2 * planes, (chip + 1) * 2 * planes)) for chip in range(count // 2)]
    return lax.all_to_all(
        chunks, ("ctx", "exp"), split_axis=0, concat_axis=0, tiled=True, axis_index_groups=groups
    )


def swap(value):
    count = lax.axis_size("ctx")
    return lax.ppermute(value, "ctx", [(i, i ^ 1) for i in range(count)])


def dot(left, right):
    return jnp.dot(left, right, preferred_element_type=f32)


def dot_last(left, right):
    return lax.dot_general(left, right, (((1,), (1,)), ((), ())), preferred_element_type=f32)


def iota(shape, dim):
    return lax.broadcasted_iota(jnp.int32, shape, dim)


def local_kernel(kernel, out_shape, *operands, spaces=None, grant=6, **kwargs):
    spaces = spaces or [pltpu.VMEM] * len(operands)
    return pl.pallas_call(
        kernel,
        out_shape=out_shape,
        in_specs=[pl.BlockSpec(memory_space=space) for space in spaces],
        out_specs=jax.tree.map(lambda _: pl.BlockSpec(memory_space=pltpu.VMEM), out_shape),
        compiler_params=pltpu.CompilerParams(vmem_limit_bytes=grant * 1024 * 1024),
        **kwargs,
    )(*operands)


def column(values):
    group, run = values.shape
    tokens = group * run
    spread = (iota((tokens, group), 0) // run == iota((tokens, group), 1)).astype(f32)
    inside = iota((tokens, run), 0) % run == iota((tokens, run), 1)
    values = jnp.dot(spread, values, preferred_element_type=f32, precision=lax.Precision.HIGHEST)
    return jnp.sum(jnp.where(inside, values, 0.0), axis=1, keepdims=True)


def side_kernel(place_ref, gate_ref, gain_ref, ends_ref, out_ref, gains_ref, seen_ref, seen_pair_ref):
    out_ref[...] = jnp.broadcast_to(column(gate_ref[...]), out_ref.shape)
    gains_ref[...] = jnp.broadcast_to(gain_ref[...], gains_ref.shape)
    shard, core = place_ref[0], place_ref[1]
    local, count = seen_ref.shape
    shards = ends_ref.shape[0]
    ends = ends_ref[...].astype(f32)
    query = (shard * local + iota((local, count), 0)).astype(f32)
    planes = local // 8
    chip, rest = iota((count, 1), 0) // (2 * planes), iota((count, 1), 0) % (2 * planes)
    run = jnp.where(rest >= planes, shard // BLOCK, 0)
    hidden = (rest >= planes) & (shard // BLOCK == 0)
    key_shard = run * BLOCK + chip // 4
    chosen = (iota((count, shards), 1) == key_shard).astype(f32)
    chosen = jnp.dot(chosen, ends, preferred_element_type=f32, precision=lax.Precision.HIGHEST)
    for part, ref in ((core, seen_ref), (1 - core, seen_pair_ref)):
        row = rest % planes * 8 + chip % 4 * 2 + part
        end = jnp.sum(jnp.where(iota((count, local), 1) == row, chosen, 0.0), axis=1, keepdims=True)
        end = jnp.where(hidden, -1.0, end)
        index = (key_shard * local + row).astype(f32)
        end = jnp.transpose(jnp.broadcast_to(end, (count, local)))
        index = jnp.transpose(jnp.broadcast_to(index, (count, local)))
        ref[...] = ((index <= query) & (query <= end)).astype(f32)


def routing_kernel(core_ref, expert_ref, placed_ref, table_ref):
    core = core_ref[0].astype(f32)
    expert = column(expert_ref[...])
    tokens = expert.shape[0]
    lane = iota((tokens, 128), 1).astype(f32)
    picked = expert == lane
    earlier = (iota((tokens, tokens), 1) < iota((tokens, tokens), 0)).astype(bf16)
    rank = dot(earlier, picked.astype(bf16))
    rank = jnp.sum(jnp.where(picked, rank, 0.0), axis=1, keepdims=True)

    count = placed_ref.shape[0]
    part = jnp.where(rank >= PART, 1.0, 0.0)
    valid = (expert >= 0) & (rank < CAP)
    slot = expert * PAD + rank - part * PART
    slot_rows = jnp.where(valid, part * (count // 2) + slot, -1.0)
    slot_rows = jnp.transpose(jnp.broadcast_to(slot_rows, (tokens, count)))
    placed_ref[...] = (slot_rows == iota((count, tokens), 0).astype(f32)).astype(bf16)
    wanted = jnp.where(lane == 0, core, 1.0 - core)
    table_ref[...] = jnp.where(valid & (part == wanted), slot, -1.0)


def dispatch_kernel(placed_ref, rows_ref, out_ref):
    placed = placed_ref[...]
    width = rows_ref.shape[1]
    out_ref[:, width:] = jnp.zeros((placed.shape[0], WIDE - width), bf16)
    out_ref[:, :width] = dot(placed, rows_ref[...]).astype(bf16)


def slot_choice(rows, columns, half, flip):
    wide, narrow = (1, 0) if not flip else (0, 1)
    padded, packed = iota((rows, columns), wide), iota((rows, columns), narrow)
    packed_place = packed // PART * PAD + packed % PART
    return ((padded == packed_place) & (packed < half)).astype(bf16)


def packed_kernel(half, core_ref, received_ref, gain_ref, gain_pair_ref, own_ref, pair_ref, square_ref):
    core = core_ref[0]
    width = gain_ref.shape[1]
    choice = slot_choice(128, received_ref.shape[1], half, False)
    squares = 0.0
    for part, gains, ref in ((core, gain_ref, own_ref), (1 - core, gain_pair_ref, pair_ref)):
        rows = dot(choice, received_ref[part])
        ref[...] = (rows[:half, :width] * gains[0:1, :]).astype(bf16)
        squares += jnp.sum(rows * rows, axis=1, keepdims=True)
    squares = jnp.transpose(jnp.broadcast_to(squares, (128, 128)))[:16]
    high = squares.astype(bf16).astype(f32)
    sub = iota((16, 128), 0)
    square_ref[...] = jnp.where(sub == 0, high, jnp.where(sub == 1, squares - high, 0.0)).astype(bf16)


def gate_up_kernel(own_ref, pair_ref, square_ref, gate_own, gate_pair, up_own, up_pair, out_ref):
    half = own_ref.shape[0]
    owners, _, lanes = out_ref.shape
    own, pair, squares = own_ref[...], pair_ref[...], square_ref[...]
    group = 4
    for first in range(0, owners, group):
        span = slice(first * lanes, (first + group) * lanes)
        gate = (dot(own, gate_own[:, span]) + dot(pair, gate_pair[:, span])).astype(bf16)
        up = (dot(own, up_own[:, span]) + dot(pair, up_pair[:, span])).astype(bf16)
        for at in range(group):
            lane = slice(at * lanes, (at + 1) * lanes)
            out_ref[first + at, :half] = gate[:, lane]
            out_ref[first + at, half : 2 * half] = up[:, lane]
            out_ref[first + at, 2 * half :] = squares


def hidden_unit_kernel(half, partial_ref, out_ref):
    total = jnp.sum(partial_ref[...].astype(f32), axis=0)
    squares = total[2 * half : 2 * half + 1] + total[2 * half + 1 : 2 * half + 2]
    lanes = squares.shape[1]
    scale = lax.rsqrt(squares / D + norm_eps)
    scale = jnp.transpose(jnp.broadcast_to(scale, (lanes, lanes)))[:half]
    gate = total[:half] * scale
    up = total[half : 2 * half] * scale
    units = (gate / (1.0 + jnp.exp(-gate)) * up).astype(bf16)
    for owner in range(out_ref.shape[0]):
        out_ref[owner] = units


def combine_kernel(returned_ref, table_ref, gate_ref, rows_ref, own_ref, pair_ref, out_ref):
    tokens, width = rows_ref.shape
    padded = returned_ref.shape[0]
    slot, gate = table_ref[:, 0:1], gate_ref[:, 0:1]
    choice = (slot == iota((tokens, padded), 1).astype(f32)).astype(bf16)
    moe = dot(choice, returned_ref[...]) * gate
    next_own = (rows_ref[...].astype(f32) + moe[:, :width]).astype(bf16)
    next_pair = moe[:, WIDE : WIDE + width].astype(bf16)
    target, source = iota((tokens, tokens), 0), iota((tokens, tokens), 1)
    run = GROUPS * BLOCK
    rest = target % (tokens // BLOCK)
    wanted = rest // GROUPS * run + rest % GROUPS * BLOCK + target // (tokens // BLOCK)
    order = (source == wanted).astype(bf16)
    own = dot(order, next_own).astype(bf16)
    pair = dot(order, next_pair).astype(bf16)
    out_ref[...] = (dot(own, own_ref[...]) + dot(pair, pair_ref[...])).astype(bf16)


def latent_kernel(part_ref, gain_ref, out_ref):
    raw = jnp.sum(part_ref[...].astype(f32), axis=0)
    scale = lax.rsqrt(jnp.mean(raw * raw, axis=1, keepdims=True) + norm_eps)
    latent = (raw * scale * gain_ref[...]).astype(bf16)
    for plane in range(out_ref.shape[0]):
        out_ref[plane] = latent


def key_kernel(plane_ref, out_ref):
    chips, rows, _ = out_ref.shape
    planes = rows // 2
    total = plane_ref.shape[0]
    target, source = iota((total, total), 0), iota((total, total), 1)
    order = (source == target % planes * GROUPS + target // planes).astype(bf16)
    ordered = dot(order, plane_ref[...]).astype(bf16)
    for chip in range(chips):
        run = chip // (BLOCK // 2)
        out_ref[chip, :planes] = ordered[:planes]
        out_ref[chip, planes:] = ordered[run * planes : (run + 1) * planes]


def next_kernel(returned_ref, rest_ref, table_ref, gate_ref, rows_ref, out_ref):
    tokens, width = rows_ref.shape
    padded = returned_ref.shape[0]
    lane = iota((tokens, padded), 1).astype(f32)
    moe = dot((table_ref[:, 0:1] == lane).astype(bf16), returned_ref[:, :width])
    moe += dot((table_ref[:, 1:2] == lane).astype(bf16), rest_ref[:, :width])
    out_ref[...] = (rows_ref[...].astype(f32) + moe * gate_ref[:, 0:1]).astype(bf16)


def attend(queries_ref, keys_ref, seen_ref):
    keys = keys_ref[...]
    seen = jnp.concatenate([seen_ref[...]] * (queries_ref.shape[0] // seen_ref.shape[0]), axis=0) > 0
    scores = jnp.where(seen, dot_last(queries_ref[...], keys) * score_scale, neg_fill)
    top = jnp.max(scores, axis=1, keepdims=True)
    weights = jnp.where(seen, jnp.exp(scores - top), 0.0)
    return top, jnp.sum(weights, axis=1, keepdims=True), dot(weights.astype(bf16), keys)


def first_kernel(queries_ref, keys_ref, seen_ref, stats_ref, mixed_ref):
    top, denom, mixed = attend(queries_ref, keys_ref, seen_ref)
    stats_ref[...] = jnp.where(iota(stats_ref.shape, 1) == 0, top, denom)
    mixed_ref[...] = mixed


def second_kernel(queries_ref, keys_ref, seen_ref, stats_ref, mixed_ref, out_ref):
    top, denom, mixed = attend(queries_ref, keys_ref, seen_ref)
    first_top, first_denom = stats_ref[:, 0:1], stats_ref[:, 1:2]
    most = jnp.maximum(top, first_top)
    share, first_share = jnp.exp(top - most), jnp.exp(first_top - most)
    total = denom * share + first_denom * first_share
    out_ref[...] = (mixed * (share / total) + mixed_ref[...] * (first_share / total)).astype(bf16)


def body(
    hidden,
    routes,
    gates,
    moe_gain,
    gate_weight,
    up_weight,
    down_weight,
    latent_weight,
    latent_gain,
    queries,
    subtree_end,
):
    row_group, shard_count, width = hidden.shape
    tokens = row_group * shard_count
    exp_count = lax.axis_size("exp")
    ctx_count = lax.axis_size("ctx")
    chips = ctx_count // 2
    half = exp_count * PART
    padded = exp_count * PAD
    hidden_width = gate_weight.shape[2]
    lanes = hidden_width // chips
    latent_width = latent_weight.shape[1]

    rows = hidden.reshape(tokens, width)
    core = lax.rem(lax.axis_index("ctx"), 2)

    shape = jax.ShapeDtypeStruct
    near = routes < exp_count
    expert = jnp.max(jnp.where(near, routes, -1), axis=2).astype(f32)
    both = 2 * padded
    placed, table = local_kernel(
        routing_kernel,
        (shape((both, tokens), bf16), shape((tokens, 128), f32)),
        core.reshape(1),
        expert,
        spaces=[pltpu.SMEM, pltpu.VMEM],
    )
    dispatched = local_kernel(dispatch_kernel, shape((both, WIDE), bf16), placed, rows)
    own = (gate_weight[0], up_weight[0], down_weight[0].T, latent_weight, moe_gain)
    late = (gates, latent_gain, subtree_end)
    dispatched, own, late = lax.optimization_barrier((dispatched, own, late))
    gate = jnp.sum(jnp.where(near, late[0], 0.0), axis=2)
    local, heads = queries.shape[:2]
    sight = shape((local, chips * 2 * exp_count), f32)
    gate, latent_gains, seen, seen_pair = local_kernel(
        side_kernel,
        (shape((tokens, 128), f32), shape((8, latent_width), f32), sight, sight),
        jnp.stack([lax.axis_index("ctx"), core]),
        gate,
        late[1][None, :],
        late[2].reshape(ctx_count, local),
        spaces=[pltpu.SMEM] + [pltpu.VMEM] * 3,
    )
    gate_own, up_own, down_own, _, gain_own = own
    gain_own = jnp.broadcast_to(gain_own[None, :], (8, width))
    gate_pair, up_pair, down_pair, latent_pair, gain_pair = [swap(value) for value in own[:4] + (gain_own,)]
    received = exchange_pairs(dispatched.reshape(2 * exp_count, PAD, WIDE)).reshape(2, padded, WIDE)

    packed = local_kernel(
        lambda *refs: packed_kernel(half, *refs),
        (shape((half, width), bf16), shape((half, width), bf16), shape((16, 128), bf16)),
        core.reshape(1),
        received,
        gain_own,
        gain_pair,
        spaces=[pltpu.SMEM] + [pltpu.VMEM] * 3,
        cost_estimate=pl.CostEstimate(flops=COST, bytes_accessed=COST, transcendentals=0),
    )
    partial = local_kernel(
        gate_up_kernel, shape((chips, 2 * half + 16, lanes), bf16), *packed, gate_own, gate_pair, up_own, up_pair
    )
    partial = exchange_chips(partial)
    units = local_kernel(
        lambda *refs: hidden_unit_kernel(half, *refs), shape((chips, half, lanes), bf16), partial
    )
    spread = exchange_chips(units).transpose(1, 0, 2).reshape(half, hidden_width)

    fill = ((0, 0), (0, WIDE - width))
    expert_out = jnp.concatenate(
        [
            jnp.pad(lax.dot_general(spread, w, (((1,), (1,)), ((), ())), preferred_element_type=f32).astype(bf16), fill)
            for w in (down_own, down_pair)
        ],
        axis=1,
    )
    expert_out = jnp.pad(expert_out.reshape(exp_count, PART, 2 * WIDE), ((0, 0), (0, PAD - PART), (0, 0)))
    returned = exchange(expert_out, "exp").reshape(padded, 2 * WIDE)
    returned_rest = swap(returned[:, WIDE:])
    latent_part = local_kernel(
        combine_kernel,
        jax.ShapeDtypeStruct((tokens, latent_width), bf16),
        returned,
        table,
        gate,
        rows,
        latent_weight,
        latent_pair,
    )
    latent_part = exchange(latent_part.reshape(ctx_count, GROUPS, latent_width), "ctx")
    latent = local_kernel(
        latent_kernel, shape((exp_count, GROUPS, latent_width), bf16), latent_part, latent_gains
    )
    latent, returned_rest = lax.optimization_barrier((latent, returned_rest))
    plane = exchange(latent, "exp").reshape(exp_count * GROUPS, latent_width)
    next_rows = local_kernel(
        next_kernel, shape(rows.shape, bf16), returned, returned_rest, table, gate, rows
    )
    queries = queries.transpose(1, 0, 2).reshape(heads * local, latent_width)
    chunks = local_kernel(key_kernel, shape((chips, 2 * exp_count, latent_width), bf16), plane)
    chunks, next_rows, queries = lax.optimization_barrier((chunks, next_rows, queries))
    keys = exchange_chips(chunks).reshape(chips * 2 * exp_count, latent_width)
    keys_pair = swap(keys)

    first = local_kernel(
        first_kernel,
        (shape((heads * local, 128), f32), shape((heads * local, latent_width), f32)),
        queries,
        keys,
        seen,
        grant=16,
    )
    attn_out = local_kernel(
        second_kernel,
        shape((heads * local, latent_width), bf16),
        queries,
        keys_pair,
        seen_pair,
        *first,
        grant=16,
    )
    attn_out = attn_out.reshape(heads, local, latent_width).transpose(1, 0, 2)
    return (next_rows.reshape(hidden.shape), attn_out)


def solution(mesh):
    return jax.shard_map(
        body,
        mesh=mesh,
        in_specs=(
            P("exp", None, "ctx"),
            P("exp", None, None),
            P("exp", None, None),
            P("ctx"),
            P("exp", "ctx", None),
            P("exp", "ctx", None),
            P("exp", None, "ctx"),
            P("ctx", None),
            P(),
            P("ctx", "exp", None),
            P(),
        ),
        out_specs=(P("exp", None, "ctx"), P("ctx", "exp", None)),
        check_vma=False,
    )
```

```python
import jax
import jax.numpy as jnp
from jax import lax
from jax.experimental import pallas as pl
from jax.experimental.pallas import tpu as pltpu
from jax.sharding import PartitionSpec as P

D = 7168
TOP = 8
CAP = 12
PART = 6
PAD = 8
WIDE = 256
GROUPS = 8
BLOCK = 4
COST = 5_000_000_000


score_scale = 192 ** (-0.5)
norm_eps = 1e-06
neg_fill = -1e30
bf16, f32 = jnp.bfloat16, jnp.float32


def exchange(chunks, axis):
    return lax.all_to_all(chunks, axis, split_axis=0, concat_axis=0, tiled=True)


def exchange_chips(chunks):
    count = lax.axis_size("ctx")
    groups = [list(range(core, count, 2)) for core in range(2)]
    return lax.all_to_all(
        chunks, "ctx", split_axis=0, concat_axis=0, tiled=True, axis_index_groups=groups
    )


def exchange_pairs(chunks):
    count, planes = lax.axis_size("ctx"), lax.axis_size("exp")
    groups = [list(range(chip * 2 * planes, (chip + 1) * 2 * planes)) for chip in range(count // 2)]
    return lax.all_to_all(
        chunks, ("ctx", "exp"), split_axis=0, concat_axis=0, tiled=True, axis_index_groups=groups
    )


def swap(value):
    count = lax.axis_size("ctx")
    return lax.ppermute(value, "ctx", [(i, i ^ 1) for i in range(count)])


def dot(left, right):
    return jnp.dot(left, right, preferred_element_type=f32)


def dot_last(left, right):
    return lax.dot_general(left, right, (((1,), (1,)), ((), ())), preferred_element_type=f32)


def iota(shape, dim):
    return lax.broadcasted_iota(jnp.int32, shape, dim)


def local_kernel(kernel, out_shape, *operands, spaces=None, grant=6, **kwargs):
    spaces = spaces or [pltpu.VMEM] * len(operands)
    return pl.pallas_call(
        kernel,
        out_shape=out_shape,
        in_specs=[pl.BlockSpec(memory_space=space) for space in spaces],
        out_specs=jax.tree.map(lambda _: pl.BlockSpec(memory_space=pltpu.VMEM), out_shape),
        compiler_params=pltpu.CompilerParams(vmem_limit_bytes=grant * 1024 * 1024),
        **kwargs,
    )(*operands)


def column(values):
    group, run = values.shape
    tokens = group * run
    spread = (iota((tokens, group), 0) // run == iota((tokens, group), 1)).astype(f32)
    inside = iota((tokens, run), 0) % run == iota((tokens, run), 1)
    values = jnp.dot(spread, values, preferred_element_type=f32, precision=lax.Precision.HIGHEST)
    return jnp.sum(jnp.where(inside, values, 0.0), axis=1, keepdims=True)


def side_kernel(place_ref, gate_ref, gain_ref, ends_ref, out_ref, gains_ref, seen_ref, seen_pair_ref):
    out_ref[...] = jnp.broadcast_to(column(gate_ref[...]), out_ref.shape)
    gains_ref[...] = jnp.broadcast_to(gain_ref[...], gains_ref.shape)
    shard, core = place_ref[0], place_ref[1]
    local, count = seen_ref.shape
    shards = ends_ref.shape[0]
    ends = ends_ref[...].astype(f32)
    query = (shard * local + iota((local, count), 0)).astype(f32)
    planes = local // 8
    chip, rest = iota((count, 1), 0) // (2 * planes), iota((count, 1), 0) % (2 * planes)
    run = jnp.where(rest >= planes, shard // BLOCK, 0)
    hidden = (rest >= planes) & (shard // BLOCK == 0)
    key_shard = run * BLOCK + chip // 4
    chosen = (iota((count, shards), 1) == key_shard).astype(f32)
    chosen = jnp.dot(chosen, ends, preferred_element_type=f32, precision=lax.Precision.HIGHEST)
    for part, ref in ((core, seen_ref), (1 - core, seen_pair_ref)):
        row = rest % planes * 8 + chip % 4 * 2 + part
        end = jnp.sum(jnp.where(iota((count, local), 1) == row, chosen, 0.0), axis=1, keepdims=True)
        end = jnp.where(hidden, -1.0, end)
        index = (key_shard * local + row).astype(f32)
        end = jnp.transpose(jnp.broadcast_to(end, (count, local)))
        index = jnp.transpose(jnp.broadcast_to(index, (count, local)))
        ref[...] = ((index <= query) & (query <= end)).astype(f32)


def dispatch_kernel(exp_count, core_ref, routes_hbm, rows_hbm, table_ref, out_ref, routes_ref, rows_ref, sems):
    routes_copy = pltpu.make_async_copy(routes_hbm, routes_ref, sems.at[0])
    copy = pltpu.make_async_copy(rows_hbm, rows_ref, sems.at[1])
    routes_copy.start()
    copy.start()
    core = core_ref[0].astype(f32)
    routes_copy.wait()
    routes = routes_ref[...]
    expert = column(jnp.max(jnp.where(routes < exp_count, routes, -1), axis=1).astype(f32))
    tokens = expert.shape[0]
    lane = iota((tokens, 128), 1).astype(f32)
    picked = expert == lane
    earlier = (iota((tokens, tokens), 1) < iota((tokens, tokens), 0)).astype(bf16)
    rank = dot(earlier, picked.astype(bf16))
    rank = jnp.sum(jnp.where(picked, rank, 0.0), axis=1, keepdims=True)

    count = out_ref.shape[0]
    part = jnp.where(rank >= PART, 1.0, 0.0)
    valid = (expert >= 0) & (rank < CAP)
    slot = expert * PAD + rank - part * PART
    slot_rows = jnp.where(valid, part * (count // 2) + slot, -1.0)
    slot_rows = jnp.transpose(jnp.broadcast_to(slot_rows, (tokens, count)))
    placed = (slot_rows == iota((count, tokens), 0).astype(f32)).astype(bf16)
    wanted = jnp.where(lane == 0, core, 1.0 - core)
    table_ref[...] = jnp.where(valid & (part == wanted), slot, -1.0)
    width = rows_ref.shape[1]
    out_ref[:, width:] = jnp.zeros((count, WIDE - width), bf16)
    copy.wait()
    out_ref[:, :width] = dot(placed, rows_ref[...]).astype(bf16)


def slot_choice(rows, columns, half, flip):
    wide, narrow = (1, 0) if not flip else (0, 1)
    padded, packed = iota((rows, columns), wide), iota((rows, columns), narrow)
    packed_place = packed // PART * PAD + packed % PART
    return ((padded == packed_place) & (packed < half)).astype(bf16)


def packed_kernel(half, core_ref, received_ref, gain_ref, gain_pair_ref, own_ref, pair_ref, square_ref):
    core = core_ref[0]
    width = gain_ref.shape[1]
    choice = slot_choice(128, received_ref.shape[1], half, False)
    squares = 0.0
    for part, gains, ref in ((core, gain_ref, own_ref), (1 - core, gain_pair_ref, pair_ref)):
        rows = dot(choice, received_ref[part])
        ref[...] = (rows[:half, :width] * gains[0:1, :]).astype(bf16)
        squares += jnp.sum(rows * rows, axis=1, keepdims=True)
    squares = jnp.transpose(jnp.broadcast_to(squares, (128, 128)))[:16]
    high = squares.astype(bf16).astype(f32)
    sub = iota((16, 128), 0)
    square_ref[...] = jnp.where(sub == 0, high, jnp.where(sub == 1, squares - high, 0.0)).astype(bf16)


def gate_up_kernel(own_ref, pair_ref, square_ref, gate_own, gate_pair, up_own, up_pair, out_ref):
    half = own_ref.shape[0]
    owners, _, lanes = out_ref.shape
    own, pair, squares = own_ref[...], pair_ref[...], square_ref[...]
    group = 4
    for first in range(0, owners, group):
        span = slice(first * lanes, (first + group) * lanes)
        gate = (dot(own, gate_own[:, span]) + dot(pair, gate_pair[:, span])).astype(bf16)
        up = (dot(own, up_own[:, span]) + dot(pair, up_pair[:, span])).astype(bf16)
        for at in range(group):
            lane = slice(at * lanes, (at + 1) * lanes)
            out_ref[first + at, :half] = gate[:, lane]
            out_ref[first + at, half : 2 * half] = up[:, lane]
            out_ref[first + at, 2 * half :] = squares


def hidden_unit_kernel(half, partial_ref, out_ref):
    total = jnp.sum(partial_ref[...].astype(f32), axis=0)
    squares = total[2 * half : 2 * half + 1] + total[2 * half + 1 : 2 * half + 2]
    lanes = squares.shape[1]
    scale = lax.rsqrt(squares / D + norm_eps)
    scale = jnp.transpose(jnp.broadcast_to(scale, (lanes, lanes)))[:half]
    gate = total[:half] * scale
    up = total[half : 2 * half] * scale
    units = (gate / (1.0 + jnp.exp(-gate)) * up).astype(bf16)
    for owner in range(out_ref.shape[0]):
        out_ref[owner] = units


def combine_kernel(returned_ref, table_ref, gate_ref, rows_ref, own_ref, pair_ref, out_ref):
    tokens, width = rows_ref.shape
    padded = returned_ref.shape[0]
    slot, gate = table_ref[:, 0:1], gate_ref[:, 0:1]
    choice = (slot == iota((tokens, padded), 1).astype(f32)).astype(bf16)
    moe = dot(choice, returned_ref[...]) * gate
    next_own = (rows_ref[...].astype(f32) + moe[:, :width]).astype(bf16)
    next_pair = moe[:, WIDE : WIDE + width].astype(bf16)
    target, source = iota((tokens, tokens), 0), iota((tokens, tokens), 1)
    run = GROUPS * BLOCK
    rest = target % (tokens // BLOCK)
    wanted = rest // GROUPS * run + rest % GROUPS * BLOCK + target // (tokens // BLOCK)
    order = (source == wanted).astype(bf16)
    own = dot(order, next_own).astype(bf16)
    pair = dot(order, next_pair).astype(bf16)
    out_ref[...] = (dot(own, own_ref[...]) + dot(pair, pair_ref[...])).astype(bf16)


def latent_kernel(part_ref, gain_ref, out_ref):
    raw = jnp.sum(part_ref[...].astype(f32), axis=0)
    scale = lax.rsqrt(jnp.mean(raw * raw, axis=1, keepdims=True) + norm_eps)
    latent = (raw * scale * gain_ref[...]).astype(bf16)
    for plane in range(out_ref.shape[0]):
        out_ref[plane] = latent


def key_kernel(plane_ref, out_ref):
    chips, rows, _ = out_ref.shape
    planes = rows // 2
    total = plane_ref.shape[0]
    target, source = iota((total, total), 0), iota((total, total), 1)
    order = (source == target % planes * GROUPS + target // planes).astype(bf16)
    ordered = dot(order, plane_ref[...]).astype(bf16)
    for chip in range(chips):
        run = chip // (BLOCK // 2)
        out_ref[chip, :planes] = ordered[:planes]
        out_ref[chip, planes:] = ordered[run * planes : (run + 1) * planes]


def next_kernel(returned_ref, rest_ref, table_ref, gate_ref, rows_ref, out_ref):
    tokens, width = rows_ref.shape
    padded = returned_ref.shape[0]
    lane = iota((tokens, padded), 1).astype(f32)
    moe = dot((table_ref[:, 0:1] == lane).astype(bf16), returned_ref[:, :width])
    moe += dot((table_ref[:, 1:2] == lane).astype(bf16), rest_ref[:, :width])
    out_ref[...] = (rows_ref[...].astype(f32) + moe * gate_ref[:, 0:1]).astype(bf16)


def attend(queries_ref, keys_ref, seen_ref):
    keys = keys_ref[...]
    seen = jnp.concatenate([seen_ref[...]] * (queries_ref.shape[0] // seen_ref.shape[0]), axis=0) > 0
    scores = jnp.where(seen, dot_last(queries_ref[...], keys) * score_scale, neg_fill)
    top = jnp.max(scores, axis=1, keepdims=True)
    weights = jnp.where(seen, jnp.exp(scores - top), 0.0)
    return top, jnp.sum(weights, axis=1, keepdims=True), dot(weights.astype(bf16), keys)


def first_kernel(queries_ref, keys_ref, seen_ref, stats_ref, mixed_ref):
    top, denom, mixed = attend(queries_ref, keys_ref, seen_ref)
    stats_ref[...] = jnp.where(iota(stats_ref.shape, 1) == 0, top, denom)
    mixed_ref[...] = mixed


def second_kernel(queries_ref, keys_ref, seen_ref, stats_ref, mixed_ref, out_ref):
    top, denom, mixed = attend(queries_ref, keys_ref, seen_ref)
    first_top, first_denom = stats_ref[:, 0:1], stats_ref[:, 1:2]
    most = jnp.maximum(top, first_top)
    share, first_share = jnp.exp(top - most), jnp.exp(first_top - most)
    total = denom * share + first_denom * first_share
    out_ref[...] = (mixed * (share / total) + mixed_ref[...] * (first_share / total)).astype(bf16)


def body(
    hidden,
    routes,
    gates,
    moe_gain,
    gate_weight,
    up_weight,
    down_weight,
    latent_weight,
    latent_gain,
    queries,
    subtree_end,
):
    row_group, shard_count, width = hidden.shape
    tokens = row_group * shard_count
    exp_count = lax.axis_size("exp")
    ctx_count = lax.axis_size("ctx")
    chips = ctx_count // 2
    half = exp_count * PART
    padded = exp_count * PAD
    hidden_width = gate_weight.shape[2]
    lanes = hidden_width // chips
    latent_width = latent_weight.shape[1]

    rows = hidden.reshape(tokens, width)
    core = lax.rem(lax.axis_index("ctx"), 2)

    shape = jax.ShapeDtypeStruct
    near = routes < exp_count
    routes_by_top = routes.transpose(0, 2, 1)
    both = 2 * padded
    both = 2 * padded
    table, dispatched = local_kernel(
        lambda *refs: dispatch_kernel(exp_count, *refs),
        (shape((tokens, 128), f32), shape((both, WIDE), bf16)),
        core.reshape(1),
        routes_by_top,
        rows,
        spaces=[pltpu.SMEM, pl.ANY, pl.ANY],
        grant=60,
        scratch_shapes=[
            pltpu.VMEM(routes_by_top.shape, jnp.int32),
            pltpu.VMEM(rows.shape, bf16),
            pltpu.SemaphoreType.DMA((2,)),
        ],
    )
    own = (gate_weight[0], up_weight[0], down_weight[0].T, latent_weight, moe_gain)
    late = (gates, latent_gain, subtree_end)
    dispatched, own, late = lax.optimization_barrier((dispatched, own, late))
    gate = jnp.sum(jnp.where(near, late[0], 0.0), axis=2)
    local, heads = queries.shape[:2]
    sight = shape((local, chips * 2 * exp_count), f32)
    gate, latent_gains, seen, seen_pair = local_kernel(
        side_kernel,
        (shape((tokens, 128), f32), shape((8, latent_width), f32), sight, sight),
        jnp.stack([lax.axis_index("ctx"), core]),
        gate,
        late[1][None, :],
        late[2].reshape(ctx_count, local),
        spaces=[pltpu.SMEM] + [pltpu.VMEM] * 3,
    )
    gate_own, up_own, down_own, _, gain_own = own
    gain_own = jnp.broadcast_to(gain_own[None, :], (8, width))
    gate_pair, up_pair, down_pair, latent_pair, gain_pair = [swap(value) for value in own[:4] + (gain_own,)]
    received = exchange_pairs(dispatched.reshape(2 * exp_count, PAD, WIDE)).reshape(2, padded, WIDE)

    packed = local_kernel(
        lambda *refs: packed_kernel(half, *refs),
        (shape((half, width), bf16), shape((half, width), bf16), shape((16, 128), bf16)),
        core.reshape(1),
        received,
        gain_own,
        gain_pair,
        spaces=[pltpu.SMEM] + [pltpu.VMEM] * 3,
        cost_estimate=pl.CostEstimate(flops=COST, bytes_accessed=COST, transcendentals=0),
    )
    partial = local_kernel(
        gate_up_kernel, shape((chips, 2 * half + 16, lanes), bf16), *packed, gate_own, gate_pair, up_own, up_pair
    )
    partial = exchange_chips(partial)
    units = local_kernel(
        lambda *refs: hidden_unit_kernel(half, *refs), shape((chips, half, lanes), bf16), partial
    )
    spread = exchange_chips(units).transpose(1, 0, 2).reshape(half, hidden_width)

    fill = ((0, 0), (0, WIDE - width))
    expert_out = jnp.concatenate(
        [
            jnp.pad(lax.dot_general(spread, w, (((1,), (1,)), ((), ())), preferred_element_type=f32).astype(bf16), fill)
            for w in (down_own, down_pair)
        ],
        axis=1,
    )
    expert_out = jnp.pad(expert_out.reshape(exp_count, PART, 2 * WIDE), ((0, 0), (0, PAD - PART), (0, 0)))
    returned = exchange(expert_out, "exp").reshape(padded, 2 * WIDE)
    returned_rest = swap(returned[:, WIDE:])
    latent_part = local_kernel(
        combine_kernel,
        jax.ShapeDtypeStruct((tokens, latent_width), bf16),
        returned,
        table,
        gate,
        rows,
        latent_weight,
        latent_pair,
    )
    latent_part = exchange(latent_part.reshape(ctx_count, GROUPS, latent_width), "ctx")
    latent = local_kernel(
        latent_kernel, shape((exp_count, GROUPS, latent_width), bf16), latent_part, latent_gains
    )
    latent, returned_rest = lax.optimization_barrier((latent, returned_rest))
    plane = exchange(latent, "exp").reshape(exp_count * GROUPS, latent_width)
    next_rows = local_kernel(
        next_kernel, shape(rows.shape, bf16), returned, returned_rest, table, gate, rows
    )
    queries = queries.transpose(1, 0, 2).reshape(heads * local, latent_width)
    chunks = local_kernel(key_kernel, shape((chips, 2 * exp_count, latent_width), bf16), plane)
    chunks, next_rows, queries = lax.optimization_barrier((chunks, next_rows, queries))
    keys = exchange_chips(chunks).reshape(chips * 2 * exp_count, latent_width)
    keys_pair = swap(keys)

    first = local_kernel(
        first_kernel,
        (shape((heads * local, 128), f32), shape((heads * local, latent_width), f32)),
        queries,
        keys,
        seen,
        grant=16,
    )
    attn_out = local_kernel(
        second_kernel,
        shape((heads * local, latent_width), bf16),
        queries,
        keys_pair,
        seen_pair,
        *first,
        grant=16,
    )
    attn_out = attn_out.reshape(heads, local, latent_width).transpose(1, 0, 2)
    return (next_rows.reshape(hidden.shape), attn_out)


def solution(mesh):
    return jax.shard_map(
        body,
        mesh=mesh,
        in_specs=(
            P("exp", None, "ctx"),
            P("exp", None, None),
            P("exp", None, None),
            P("ctx"),
            P("exp", "ctx", None),
            P("exp", "ctx", None),
            P("exp", None, "ctx"),
            P("ctx", None),
            P(),
            P("ctx", "exp", None),
            P(),
        ),
        out_specs=(P("exp", None, "ctx"), P("ctx", "exp", None)),
        check_vma=False,
    )
```

```python
import jax
import jax.numpy as jnp
from jax import lax
from jax.experimental import pallas as pl
from jax.experimental.pallas import tpu as pltpu
from jax.sharding import PartitionSpec as P

D = 7168
TOP = 8
CAP = 12
PART = 6
PAD = 8
WIDE = 256
GROUPS = 8
BLOCK = 4
ORDER = [0, 4, 8, 12, 1, 5, 9, 13, 2, 6, 10, 14, 3, 7, 11, 15]
COST = 5_000_000_000


score_scale = 192 ** (-0.5)
norm_eps = 1e-06
neg_fill = -1e30
bf16, f32 = jnp.bfloat16, jnp.float32


def exchange(chunks, axis):
    return lax.all_to_all(chunks, axis, split_axis=0, concat_axis=0, tiled=True)


def exchange_chips(chunks, order=None):
    count = lax.axis_size("ctx")
    order = order or range(count // 2)
    groups = [[2 * chip + core for chip in order] for core in range(2)]
    return lax.all_to_all(
        chunks, "ctx", split_axis=0, concat_axis=0, tiled=True, axis_index_groups=groups
    )


def exchange_pairs(chunks):
    count, planes = lax.axis_size("ctx"), lax.axis_size("exp")
    groups = [list(range(chip * 2 * planes, (chip + 1) * 2 * planes)) for chip in range(count // 2)]
    return lax.all_to_all(
        chunks, ("ctx", "exp"), split_axis=0, concat_axis=0, tiled=True, axis_index_groups=groups
    )


def swap(value):
    count = lax.axis_size("ctx")
    return lax.ppermute(value, "ctx", [(i, i ^ 1) for i in range(count)])


def dot(left, right):
    return jnp.dot(left, right, preferred_element_type=f32)


def dot_last(left, right):
    return lax.dot_general(left, right, (((1,), (1,)), ((), ())), preferred_element_type=f32)


def iota(shape, dim):
    return lax.broadcasted_iota(jnp.int32, shape, dim)


def local_kernel(kernel, out_shape, *operands, spaces=None, grant=6, **kwargs):
    spaces = spaces or [pltpu.VMEM] * len(operands)
    return pl.pallas_call(
        kernel,
        out_shape=out_shape,
        in_specs=[pl.BlockSpec(memory_space=space) for space in spaces],
        out_specs=jax.tree.map(lambda _: pl.BlockSpec(memory_space=pltpu.VMEM), out_shape),
        compiler_params=pltpu.CompilerParams(vmem_limit_bytes=grant * 1024 * 1024),
        **kwargs,
    )(*operands)


def column(values):
    group, run = values.shape
    tokens = group * run
    spread = (iota((tokens, group), 0) // run == iota((tokens, group), 1)).astype(f32)
    inside = iota((tokens, run), 0) % run == iota((tokens, run), 1)
    values = jnp.dot(spread, values, preferred_element_type=f32, precision=lax.Precision.HIGHEST)
    return jnp.sum(jnp.where(inside, values, 0.0), axis=1, keepdims=True)


def side_kernel(place_ref, gate_ref, gain_ref, ends_ref, out_ref, gains_ref, seen_ref, seen_pair_ref):
    out_ref[...] = jnp.broadcast_to(column(gate_ref[...]), out_ref.shape)
    gains_ref[...] = jnp.broadcast_to(gain_ref[...], gains_ref.shape)
    shard, core = place_ref[0], place_ref[1]
    local, count = seen_ref.shape
    shards = ends_ref.shape[0]
    ends = ends_ref[...].astype(f32)
    query = (shard * local + iota((local, count), 0)).astype(f32)
    planes = local // 8
    chip, rest = iota((count, 1), 0) // (2 * planes), iota((count, 1), 0) % (2 * planes)
    run = jnp.where(rest >= planes, shard // BLOCK, 0)
    hidden = (rest >= planes) & (shard // BLOCK == 0)
    key_shard = run * BLOCK + chip // 4
    chosen = (iota((count, shards), 1) == key_shard).astype(f32)
    chosen = jnp.dot(chosen, ends, preferred_element_type=f32, precision=lax.Precision.HIGHEST)
    for part, ref in ((core, seen_ref), (1 - core, seen_pair_ref)):
        row = rest % planes * 8 + chip % 4 * 2 + part
        end = jnp.sum(jnp.where(iota((count, local), 1) == row, chosen, 0.0), axis=1, keepdims=True)
        end = jnp.where(hidden, -1.0, end)
        index = (key_shard * local + row).astype(f32)
        end = jnp.transpose(jnp.broadcast_to(end, (count, local)))
        index = jnp.transpose(jnp.broadcast_to(index, (count, local)))
        ref[...] = ((index <= query) & (query <= end)).astype(f32)


def dispatch_kernel(exp_count, core_ref, routes_hbm, rows_hbm, table_ref, out_ref, routes_ref, rows_ref, sems):
    routes_copy = pltpu.make_async_copy(routes_hbm, routes_ref, sems.at[0])
    copy = pltpu.make_async_copy(rows_hbm, rows_ref, sems.at[1])
    routes_copy.start()
    copy.start()
    core = core_ref[0].astype(f32)
    routes_copy.wait()
    routes = routes_ref[...]
    expert = column(jnp.max(jnp.where(routes < exp_count, routes, -1), axis=1).astype(f32))
    tokens = expert.shape[0]
    lane = iota((tokens, 128), 1).astype(f32)
    picked = expert == lane
    earlier = (iota((tokens, tokens), 1) < iota((tokens, tokens), 0)).astype(bf16)
    rank = dot(earlier, picked.astype(bf16))
    rank = jnp.sum(jnp.where(picked, rank, 0.0), axis=1, keepdims=True)

    count = out_ref.shape[0]
    part = jnp.where(rank >= PART, 1.0, 0.0)
    valid = (expert >= 0) & (rank < CAP)
    slot = expert * PAD + rank - part * PART
    slot_rows = jnp.where(valid, part * (count // 2) + slot, -1.0)
    slot_rows = jnp.transpose(jnp.broadcast_to(slot_rows, (tokens, count)))
    placed = (slot_rows == iota((count, tokens), 0).astype(f32)).astype(bf16)
    wanted = jnp.where(lane == 0, core, 1.0 - core)
    table_ref[...] = jnp.where(valid & (part == wanted), slot, -1.0)
    width = rows_ref.shape[1]
    out_ref[:, width:] = jnp.zeros((count, WIDE - width), bf16)
    copy.wait()
    out_ref[:, :width] = dot(placed, rows_ref[...]).astype(bf16)


def slot_choice(rows, columns, half, flip):
    wide, narrow = (1, 0) if not flip else (0, 1)
    padded, packed = iota((rows, columns), wide), iota((rows, columns), narrow)
    packed_place = packed // PART * PAD + packed % PART
    return ((padded == packed_place) & (packed < half)).astype(bf16)


def packed_kernel(half, core_ref, received_ref, gain_ref, gain_pair_ref, own_ref, pair_ref, square_ref):
    core = core_ref[0]
    width = gain_ref.shape[1]
    choice = slot_choice(128, received_ref.shape[1], half, False)
    squares = 0.0
    for part, gains, ref in ((core, gain_ref, own_ref), (1 - core, gain_pair_ref, pair_ref)):
        rows = dot(choice, received_ref[part])
        ref[...] = (rows[:half, :width] * gains[0:1, :]).astype(bf16)
        squares += jnp.sum(rows * rows, axis=1, keepdims=True)
    squares = jnp.transpose(jnp.broadcast_to(squares, (128, 128)))[:16]
    high = squares.astype(bf16).astype(f32)
    sub = iota((16, 128), 0)
    square_ref[...] = jnp.where(sub == 0, high, jnp.where(sub == 1, squares - high, 0.0)).astype(bf16)


def gate_up_kernel(own_ref, pair_ref, square_ref, gate_own, gate_pair, up_own, up_pair, out_ref):
    half = own_ref.shape[0]
    owners, _, lanes = out_ref.shape
    own, pair, squares = own_ref[...], pair_ref[...], square_ref[...]
    group = 4
    for first in range(0, owners, group):
        span = slice(first * lanes, (first + group) * lanes)
        gate = (dot(own, gate_own[:, span]) + dot(pair, gate_pair[:, span])).astype(bf16)
        up = (dot(own, up_own[:, span]) + dot(pair, up_pair[:, span])).astype(bf16)
        for at in range(group):
            lane = slice(at * lanes, (at + 1) * lanes)
            out_ref[first + at, :half] = gate[:, lane]
            out_ref[first + at, half : 2 * half] = up[:, lane]
            out_ref[first + at, 2 * half :] = squares


def hidden_unit_kernel(half, partial_ref, out_ref):
    total = jnp.sum(partial_ref[...].astype(f32), axis=0)
    squares = total[2 * half : 2 * half + 1] + total[2 * half + 1 : 2 * half + 2]
    lanes = squares.shape[1]
    scale = lax.rsqrt(squares / D + norm_eps)
    scale = jnp.transpose(jnp.broadcast_to(scale, (lanes, lanes)))[:half]
    gate = total[:half] * scale
    up = total[half : 2 * half] * scale
    units = (gate / (1.0 + jnp.exp(-gate)) * up).astype(bf16)
    for owner in range(out_ref.shape[0]):
        out_ref[owner] = units


def combine_kernel(returned_ref, table_ref, gate_ref, rows_ref, own_ref, pair_ref, out_ref):
    tokens, width = rows_ref.shape
    padded = returned_ref.shape[0]
    slot, gate = table_ref[:, 0:1], gate_ref[:, 0:1]
    choice = (slot == iota((tokens, padded), 1).astype(f32)).astype(bf16)
    moe = dot(choice, returned_ref[...]) * gate
    next_own = (rows_ref[...].astype(f32) + moe[:, :width]).astype(bf16)
    next_pair = moe[:, WIDE : WIDE + width].astype(bf16)
    target, source = iota((tokens, tokens), 0), iota((tokens, tokens), 1)
    run = GROUPS * BLOCK
    rest = target % (tokens // BLOCK)
    wanted = rest // GROUPS * run + rest % GROUPS * BLOCK + target // (tokens // BLOCK)
    order = (source == wanted).astype(bf16)
    own = dot(order, next_own).astype(bf16)
    pair = dot(order, next_pair).astype(bf16)
    out_ref[...] = (dot(own, own_ref[...]) + dot(pair, pair_ref[...])).astype(bf16)


def latent_kernel(part_ref, gain_ref, out_ref):
    raw = jnp.sum(part_ref[...].astype(f32), axis=0)
    scale = lax.rsqrt(jnp.mean(raw * raw, axis=1, keepdims=True) + norm_eps)
    latent = (raw * scale * gain_ref[...]).astype(bf16)
    for plane in range(out_ref.shape[0]):
        out_ref[plane] = latent


def key_kernel(plane_ref, out_ref):
    chips, rows, _ = out_ref.shape
    planes = rows // 2
    total = plane_ref.shape[0]
    target, source = iota((total, total), 0), iota((total, total), 1)
    order = (source == target % planes * GROUPS + target // planes).astype(bf16)
    ordered = dot(order, plane_ref[...]).astype(bf16)
    for chip in range(chips):
        run = chip // (BLOCK // 2)
        out_ref[chip, :planes] = ordered[:planes]
        out_ref[chip, planes:] = ordered[run * planes : (run + 1) * planes]


def next_kernel(returned_ref, rest_ref, table_ref, gate_ref, rows_ref, out_ref):
    tokens, width = rows_ref.shape
    padded = returned_ref.shape[0]
    lane = iota((tokens, padded), 1).astype(f32)
    moe = dot((table_ref[:, 0:1] == lane).astype(bf16), returned_ref[:, :width])
    moe += dot((table_ref[:, 1:2] == lane).astype(bf16), rest_ref[:, :width])
    out_ref[...] = (rows_ref[...].astype(f32) + moe * gate_ref[:, 0:1]).astype(bf16)


def attend(queries_ref, keys_ref, seen_ref):
    keys = keys_ref[...]
    seen = jnp.concatenate([seen_ref[...]] * (queries_ref.shape[0] // seen_ref.shape[0]), axis=0) > 0
    scores = jnp.where(seen, dot_last(queries_ref[...], keys) * score_scale, neg_fill)
    top = jnp.max(scores, axis=1, keepdims=True)
    weights = jnp.where(seen, jnp.exp(scores - top), 0.0)
    return top, jnp.sum(weights, axis=1, keepdims=True), dot(weights.astype(bf16), keys)


def first_kernel(queries_ref, keys_ref, seen_ref, stats_ref, mixed_ref):
    top, denom, mixed = attend(queries_ref, keys_ref, seen_ref)
    stats_ref[...] = jnp.where(iota(stats_ref.shape, 1) == 0, top, denom)
    mixed_ref[...] = mixed


def second_kernel(queries_ref, keys_ref, seen_ref, stats_ref, mixed_ref, out_ref):
    top, denom, mixed = attend(queries_ref, keys_ref, seen_ref)
    first_top, first_denom = stats_ref[:, 0:1], stats_ref[:, 1:2]
    most = jnp.maximum(top, first_top)
    share, first_share = jnp.exp(top - most), jnp.exp(first_top - most)
    total = denom * share + first_denom * first_share
    out_ref[...] = (mixed * (share / total) + mixed_ref[...] * (first_share / total)).astype(bf16)


def body(
    hidden,
    routes,
    gates,
    moe_gain,
    gate_weight,
    up_weight,
    down_weight,
    latent_weight,
    latent_gain,
    queries,
    subtree_end,
):
    row_group, shard_count, width = hidden.shape
    tokens = row_group * shard_count
    exp_count = lax.axis_size("exp")
    ctx_count = lax.axis_size("ctx")
    chips = ctx_count // 2
    half = exp_count * PART
    padded = exp_count * PAD
    hidden_width = gate_weight.shape[2]
    lanes = hidden_width // chips
    latent_width = latent_weight.shape[1]

    rows = hidden.reshape(tokens, width)
    core = lax.rem(lax.axis_index("ctx"), 2)

    shape = jax.ShapeDtypeStruct
    near = routes < exp_count
    routes_by_top = routes.transpose(0, 2, 1)
    both = 2 * padded
    both = 2 * padded
    table, dispatched = local_kernel(
        lambda *refs: dispatch_kernel(exp_count, *refs),
        (shape((tokens, 128), f32), shape((both, WIDE), bf16)),
        core.reshape(1),
        routes_by_top,
        rows,
        spaces=[pltpu.SMEM, pl.ANY, pl.ANY],
        grant=60,
        scratch_shapes=[
            pltpu.VMEM(routes_by_top.shape, jnp.int32),
            pltpu.VMEM(rows.shape, bf16),
            pltpu.SemaphoreType.DMA((2,)),
        ],
    )
    own = (gate_weight[0], up_weight[0], down_weight[0].T, latent_weight, moe_gain)
    late = (gates, latent_gain, subtree_end)
    dispatched, own, late = lax.optimization_barrier((dispatched, own, late))
    gate = jnp.sum(jnp.where(near, late[0], 0.0), axis=2)
    local, heads = queries.shape[:2]
    sight = shape((local, chips * 2 * exp_count), f32)
    gate, latent_gains, seen, seen_pair = local_kernel(
        side_kernel,
        (shape((tokens, 128), f32), shape((8, latent_width), f32), sight, sight),
        jnp.stack([lax.axis_index("ctx"), core]),
        gate,
        late[1][None, :],
        late[2].reshape(ctx_count, local),
        spaces=[pltpu.SMEM] + [pltpu.VMEM] * 3,
    )
    gate_own, up_own, down_own, _, gain_own = own
    gain_own = jnp.broadcast_to(gain_own[None, :], (8, width))
    gate_pair, up_pair, down_pair, latent_pair, gain_pair = [swap(value) for value in own[:4] + (gain_own,)]
    received = exchange_pairs(dispatched.reshape(2 * exp_count, PAD, WIDE)).reshape(2, padded, WIDE)

    packed = local_kernel(
        lambda *refs: packed_kernel(half, *refs),
        (shape((half, width), bf16), shape((half, width), bf16), shape((16, 128), bf16)),
        core.reshape(1),
        received,
        gain_own,
        gain_pair,
        spaces=[pltpu.SMEM] + [pltpu.VMEM] * 3,
        cost_estimate=pl.CostEstimate(flops=COST, bytes_accessed=COST, transcendentals=0),
    )
    partial = local_kernel(
        gate_up_kernel, shape((chips, 2 * half + 16, lanes), bf16), *packed, gate_own, gate_pair, up_own, up_pair
    )
    partial = exchange_chips(partial, ORDER)
    units = local_kernel(
        lambda *refs: hidden_unit_kernel(half, *refs), shape((chips, half, lanes), bf16), partial
    )
    spread = exchange_chips(units, ORDER).transpose(1, 0, 2).reshape(half, hidden_width)

    fill = ((0, 0), (0, WIDE - width))
    expert_out = jnp.concatenate(
        [
            jnp.pad(lax.dot_general(spread, w, (((1,), (1,)), ((), ())), preferred_element_type=f32).astype(bf16), fill)
            for w in (down_own, down_pair)
        ],
        axis=1,
    )
    expert_out = jnp.pad(expert_out.reshape(exp_count, PART, 2 * WIDE), ((0, 0), (0, PAD - PART), (0, 0)))
    returned = exchange(expert_out, "exp").reshape(padded, 2 * WIDE)
    returned_rest = swap(returned[:, WIDE:])
    latent_part = local_kernel(
        combine_kernel,
        jax.ShapeDtypeStruct((tokens, latent_width), bf16),
        returned,
        table,
        gate,
        rows,
        latent_weight,
        latent_pair,
    )
    latent_part = exchange(latent_part.reshape(ctx_count, GROUPS, latent_width), "ctx")
    latent = local_kernel(
        latent_kernel, shape((exp_count, GROUPS, latent_width), bf16), latent_part, latent_gains
    )
    latent, returned_rest = lax.optimization_barrier((latent, returned_rest))
    plane = exchange(latent, "exp").reshape(exp_count * GROUPS, latent_width)
    next_rows = local_kernel(
        next_kernel, shape(rows.shape, bf16), returned, returned_rest, table, gate, rows
    )
    queries = queries.transpose(1, 0, 2).reshape(heads * local, latent_width)
    chunks = local_kernel(key_kernel, shape((chips, 2 * exp_count, latent_width), bf16), plane)
    chunks, next_rows, queries = lax.optimization_barrier((chunks, next_rows, queries))
    keys = exchange_chips(chunks).reshape(chips * 2 * exp_count, latent_width)
    keys_pair = swap(keys)

    first = local_kernel(
        first_kernel,
        (shape((heads * local, 128), f32), shape((heads * local, latent_width), f32)),
        queries,
        keys,
        seen,
        grant=16,
    )
    attn_out = local_kernel(
        second_kernel,
        shape((heads * local, latent_width), bf16),
        queries,
        keys_pair,
        seen_pair,
        *first,
        grant=16,
    )
    attn_out = attn_out.reshape(heads, local, latent_width).transpose(1, 0, 2)
    return (next_rows.reshape(hidden.shape), attn_out)


def solution(mesh):
    return jax.shard_map(
        body,
        mesh=mesh,
        in_specs=(
            P("exp", None, "ctx"),
            P("exp", None, None),
            P("exp", None, None),
            P("ctx"),
            P("exp", "ctx", None),
            P("exp", "ctx", None),
            P("exp", None, "ctx"),
            P("ctx", None),
            P(),
            P("ctx", "exp", None),
            P(),
        ),
        out_specs=(P("exp", None, "ctx"), P("ctx", "exp", None)),
        check_vma=False,
    )
```
